128 devices in a mesh: pts: 128 (over z, y, x, core).
Axes of the slice: x: 4, y: 4, z: 4, core: 2. Of those that a mesh axis runs over, the one named last changes fastest.
Arguments:
- feats: bfloat16 [3670016, 128], P('pts'), may hold values from -6 to 6
- w_first: bfloat16 [128, 128], replicated, may hold values from -0.5 to 0.5
- w_second: bfloat16 [128, 128], replicated, may hold values from -0.5 to 0.5
- w_coarse: bfloat16 [128, 128], replicated, may hold values from -0.5 to 0.5
- send_weight: bfloat16 [14336, 16, 256], P('pts'), may hold values from -1 to 1
- return_weight: bfloat16 [14336, 16, 256], P('pts'), may hold values from -2 to 2
- neighbours: int32 [14336, 16], P('pts'), may hold values from 0 to 5119, as said below
- nbr_count: int32 [14336], P('pts'), may hold values from 1 to 16, as said below
- point_count: int32 [14336], P('pts'), may hold values from 64 to 256, as said below
- cotangent: bfloat16 [3670016, 128], P('pts'), may hold values from -6 to 6
Outputs:
- grad_feats: bfloat16 [3670016, 128], P('pts')
- grad_first: float32 [128, 128], replicated
- grad_second: float32 [128, 128], replicated
- grad_coarse: float32 [128, 128], replicated
The draws below stay inside these ranges and needn't reach their ends.
Inputs may be any that keep to these rules, and one draw needn't show every extreme that they name: `neighbours`: every neighbour slot of a block of device d (blocks d * 112 to (d + 1) * 112 - 1) names an atom owned by device d - 1, d or d + 1, where device e owns atoms e * 40 to (e + 1) * 40 - 1; unused slots follow the same rule. `nbr_count`: the first block of every device uses all slots. `point_count`: the first block of every device uses all slots.
All inputs are finite; a program needn't handle non-finite values.
Results may differ from the reference program's by a relative error of at most 0.022.
Values may be sent and summed in bfloat16 or wider, within the bound.
No kernel may reach another device: no remote copies, remote signals or barrier semaphores. Data moves between devices by JAX's collectives and lax.ppermute only.
A program may use at most 192 MiB of HBM per device.

```python
import math
import jax
import jax.numpy as jnp
from jax import lax

C = 128
BLK = 256
K = 16
NB_DEV = 112
A_DEV = 40
BLOCKS = 14336
POINTS = 3670016
ATOMS = 5120


def draw_neighbours(key, part):
    key = jax.random.fold_in(key, 11)
    owner_dev = jnp.arange(BLOCKS, dtype=jnp.int32) // NB_DEV
    offsets = jax.random.randint(key, (BLOCKS, K), -A_DEV, 2 * A_DEV)
    atoms = jnp.clip(owner_dev[:, None] * A_DEV + offsets, 0, ATOMS - 1)
    atoms = atoms.at[0, 0].set(0)
    atoms = atoms.at[BLOCKS - 1, 0].set(ATOMS - 1)
    return atoms.astype(jnp.int32)


def draw_nbr_count(key, part):
    key = jax.random.fold_in(key, 23)
    counts = jax.random.randint(key, (BLOCKS,), 1, K + 1)
    counts = counts.at[::NB_DEV].set(K)
    return counts.astype(jnp.int32)


def draw_point_count(key, part):
    key = jax.random.fold_in(key, 37)
    counts = jax.random.randint(key, (BLOCKS,), BLK // 4, BLK + 1)
    counts = counts.at[::NB_DEV].set(BLK)
    return counts.astype(jnp.int32)


def block_scale(own_key, extent, shards, least, high):
    level = 1.0
    for dim, blocks in shards:
        draws = jax.random.uniform(jax.random.fold_in(jax.random.fold_in(own_key, 6), dim), (blocks,), jnp.float32, least / len(shards), high / len(shards))
        level = level * jnp.repeat(jnp.exp(draws), extent[dim] // blocks).reshape((-1,) + (1,) * (len(extent) - 1 - dim))
    return level


def bell_draw(stream_key, extent, scale, limit, pieces=(), kind=jnp.bfloat16):
    drawn = jax.random.normal(stream_key, extent, jnp.float32) * scale
    if len(pieces) > 0:
        drawn = block_scale(stream_key, extent, pieces, -0.22, 0.18) * drawn
    return jnp.clip(drawn, min=-limit, max=limit).astype(kind)


def setup_inputs(seed: int = 0) -> dict:
    key_list = jax.random.split(jax.random.key(seed), 11)
    return {
        "feats": bell_draw(key_list[0], (POINTS, C), 1.0, 6.0, ((0, 128),)),
        "w_first": bell_draw(key_list[1], (C, C), C ** -0.5, 0.5),
        "w_second": bell_draw(key_list[2], (C, C), C ** -0.5, 0.5),
        "w_coarse": bell_draw(key_list[3], (C, C), C ** -0.5, 0.5),
        "send_weight": bell_draw(key_list[4], (BLOCKS, K, BLK), 0.125, 1.0, ((0, 128),)),
        "return_weight": bell_draw(key_list[5], (BLOCKS, K, BLK), 0.3, 2.0, ((0, 128),)),
        "neighbours": draw_neighbours(jax.random.fold_in(key_list[10], 71), 0),
        "nbr_count": draw_nbr_count(jax.random.fold_in(key_list[10], 71), 0),
        "point_count": draw_point_count(jax.random.fold_in(key_list[10], 71), 0),
        "cotangent": bell_draw(key_list[9], (POINTS, C), 1.0, 6.0, ((0, 128),)),
    }


block_group = 64

def silu_slope(value):
    sig = jax.nn.sigmoid(value)
    return sig * (1.0 + value * (1.0 - sig))

def reference(feats, w_first, w_second, w_coarse, send_weight, return_weight, neighbours, nbr_count, point_count, cotangent):
    groups = BLOCKS // block_group
    slots = jnp.arange(K, dtype=jnp.int32)
    valid = (slots[None, :] < nbr_count[:, None]).astype(jnp.float32)
    spots = jnp.arange(BLK, dtype=jnp.int32)
    mask = (spots[None, :] < point_count[:, None]).astype(jnp.float32)
    feat_grp = feats.reshape(groups, block_group * BLK, C)
    cot_grp = cotangent.reshape(groups, block_group * BLK, C)
    send_grp = send_weight.reshape(groups, block_group, K, BLK)
    ret_grp = return_weight.reshape(groups, block_group, K, BLK)
    mask_grp = mask.reshape(groups, block_group * BLK)
    valid_grp = valid.reshape(groups, block_group, K)

    def outgoing(items):
        rows, sendw, retw, marks, flags, cots = items
        pre1 = jnp.dot(rows, w_first, preferred_element_type=jnp.float32)
        first = jax.nn.silu(pre1).astype(jnp.bfloat16)
        pre2 = jnp.dot(first, w_second, preferred_element_type=jnp.float32)
        point_feat = (marks[:, None] * jax.nn.silu(pre2)).astype(jnp.bfloat16).reshape(block_group, BLK, C)
        message = (jnp.einsum('gkp,gpc->gkc', sendw.astype(jnp.float32), point_feat.astype(jnp.float32)) * flags[..., None]).astype(jnp.bfloat16)
        masked = (cots.astype(jnp.float32) * marks[:, None]).astype(jnp.bfloat16).reshape(block_group, BLK, C)
        back_grad = (jnp.einsum('gkp,gpc->gkc', retw.astype(jnp.float32), masked.astype(jnp.float32)) * flags[..., None]).astype(jnp.bfloat16)
        return (message, back_grad)
    messages, back_grads = lax.map(outgoing, (feat_grp, send_grp, ret_grp, mask_grp, valid_grp, cot_grp))
    owners = neighbours.reshape(-1).astype(jnp.int32)
    coarse = jax.ops.segment_sum(messages.reshape(-1, C).astype(jnp.float32), owners, num_segments=ATOMS).astype(jnp.bfloat16)
    coarse_grad = jax.ops.segment_sum(back_grads.reshape(-1, C).astype(jnp.float32), owners, num_segments=ATOMS)
    pre_coarse = jnp.dot(coarse, w_coarse, preferred_element_type=jnp.float32)
    dpre_coarse = (coarse_grad * silu_slope(pre_coarse)).astype(jnp.bfloat16)
    grad_coarse = jnp.dot(coarse.T, dpre_coarse, preferred_element_type=jnp.float32) * (1.0 / math.sqrt(ATOMS))
    dcoarse = jnp.dot(dpre_coarse, w_coarse.T, preferred_element_type=jnp.float32).astype(jnp.bfloat16)
    message_grad = (dcoarse[owners].astype(jnp.float32) * valid.reshape(-1, 1)).astype(jnp.bfloat16)
    msg_grp = message_grad.reshape(groups, block_group, K, C)

    def incoming(items):
        rows, sendw, marks, cots, mgrad = items
        pre1 = jnp.dot(rows, w_first, preferred_element_type=jnp.float32)
        first = jax.nn.silu(pre1).astype(jnp.bfloat16)
        pre2 = jnp.dot(first, w_second, preferred_element_type=jnp.float32)
        masked = (cots.astype(jnp.float32) * marks[:, None]).astype(jnp.bfloat16)
        spread = jnp.einsum('gkp,gkc->gpc', sendw.astype(jnp.float32), mgrad.astype(jnp.float32)).reshape(-1, C)
        point_grad = masked.astype(jnp.float32) + spread
        dpre2 = (marks[:, None] * point_grad * silu_slope(pre2)).astype(jnp.bfloat16)
        grad_two = jnp.dot(first.T, dpre2, preferred_element_type=jnp.float32)
        dfirst = jnp.dot(dpre2, w_second.T, preferred_element_type=jnp.float32)
        dpre1 = (dfirst * silu_slope(pre1)).astype(jnp.bfloat16)
        grad_one = jnp.dot(rows.T, dpre1, preferred_element_type=jnp.float32)
        grad_rows = jnp.dot(dpre1, w_first.T, preferred_element_type=jnp.float32).astype(jnp.bfloat16)
        return (grad_rows, grad_one, grad_two)
    grad_rows, grad_one, grad_two = lax.map(incoming, (feat_grp, send_grp, mask_grp, cot_grp, msg_grp))
    factor = 1.0 / math.sqrt(POINTS)
    return (grad_rows.reshape(POINTS, C), lax.optimization_barrier(jnp.sum(grad_one, axis=0)) * factor, lax.optimization_barrier(jnp.sum(grad_two, axis=0)) * factor, grad_coarse)
```

```python
import math

import jax
import jax.numpy as jnp
from jax import lax
from jax.experimental import pallas as pl
from jax.experimental.pallas import tpu as pltpu
from jax.sharding import PartitionSpec as P

A_DEV = 40
A_PAD = 48
TILE = 8
HALF = TILE // 2

BF16 = jnp.bfloat16
F32 = jnp.float32


def dot(left, right):
    return jnp.dot(left, right, preferred_element_type=F32)


def dot_rows(left, right):
    return lax.dot_general(left, right, (((0,), (0,)), ((), ())), preferred_element_type=F32)


def diag_pair(weight):
    zero = jnp.zeros_like(weight)
    return jnp.concatenate(
        [jnp.concatenate([weight, zero], axis=1), jnp.concatenate([zero, weight], axis=1)], axis=0
    )


def silu_pair(half):
    up = 1.0 + jnp.tanh(half)
    value = half * up
    return value, up + value * (2.0 - up)


def select_slots(nb_ref):
    rows = lax.broadcasted_iota(jnp.int32, (3 * A_PAD, nb_ref.shape[-1]), 0)
    return jnp.where(rows == nb_ref[0], 1.0, 0.0).astype(BF16)


def outgoing_kernel(
    count_ref,
    nb_ref,
    feats_ref,
    cot_ref,
    send_ref,
    ret_ref,
    w_first_ref,
    w_second_ref,
    first_ref,
    slope1_ref,
    slope2_ref,
    to_right_ref,
    to_left_ref,
    edge_right_ref,
    edge_left_ref,
    w1_ref,
    w2_ref,
    spot_ref,
    part_ref,
):
    step = pl.program_id(0)
    block_len = send_ref.shape[1]
    slots = send_ref.shape[0] // TILE
    width = feats_ref.shape[1]

    @pl.when(step == 0)
    def _():
        w1_ref[...] = diag_pair(w_first_ref[...] * 0.5)
        w2_ref[...] = diag_pair(w_second_ref[...] * 0.5)
        spot_ref[...] = lax.broadcasted_iota(jnp.int32, spot_ref.shape, 0).astype(F32).astype(BF16)
        part_ref[...] = jnp.zeros_like(part_ref)

    lanes = lax.broadcasted_iota(jnp.int32, (slots, block_len), 1)
    lo_msg, hi_msg, lo_back, hi_back = [], [], [], []
    for pair in range(HALF):
        rows = pl.ds(pair * block_len, block_len)
        far = pl.ds((pair + HALF) * block_len, block_len)
        out = pl.ds(pl.multiple_of((step * HALF + pair) * block_len, block_len), block_len)
        counts = [count_ref[step * TILE + pair], count_ref[step * TILE + pair + HALF]]
        x = jnp.concatenate([feats_ref[rows, :], feats_ref[far, :]], axis=1)
        half1 = dot(x, w1_ref[...]).astype(BF16)
        first, slope1 = silu_pair(half1)
        first_ref[out, :] = first
        slope1_ref[out, :] = slope1
        half2 = dot(first, w2_ref[...]).astype(BF16)
        point, slope2 = silu_pair(half2)
        mask = jnp.concatenate(
            [
                jnp.clip(jnp.full((block_len, width), c.astype(F32)).astype(BF16) - spot_ref[...], 0, 1)
                for c in counts
            ],
            axis=1,
        )
        slope2_ref[out, :] = slope2 * mask

        def weights(ref):
            return jnp.concatenate(
                [
                    jnp.where(lanes < c, ref[pl.ds(b * slots, slots), :].astype(F32), 0.0).astype(BF16)
                    for b, c in zip((pair, pair + HALF), counts)
                ],
                axis=0,
            )

        cot = jnp.concatenate([cot_ref[rows, :], cot_ref[far, :]], axis=1)
        msg = dot(weights(send_ref), point)
        back = dot(weights(ret_ref), cot)
        lo_msg.append(msg[:slots, :width])
        hi_msg.append(msg[slots:, width:])
        lo_back.append(back[:slots, :width])
        hi_back.append(back[slots:, width:])
    both = jnp.concatenate(
        [jnp.concatenate(lo_msg + hi_msg, axis=0), jnp.concatenate(lo_back + hi_back, axis=0)], axis=1
    ).astype(BF16)
    part_ref[...] += dot(select_slots(nb_ref), both)

    @pl.when(step == pl.num_programs(0) - 1)
    def _():
        part = part_ref[...].astype(BF16)
        to_right_ref[...] = part[A_PAD:]
        to_left_ref[...] = part[: 2 * A_PAD]
        edge_right_ref[...] = part[2 * A_PAD :]
        edge_left_ref[...] = part[:A_PAD]


def outgoing(counts, relative, feats, cot, send, ret, w_first, w_second):
    points, width = feats.shape
    block_len = send.shape[1]
    slots = send.shape[0] // (points // block_len)
    steps = points // (TILE * block_len)
    rows = TILE * block_len
    packed = (points // 2, 2 * width)

    def whole(shape):
        return pl.BlockSpec(shape, lambda i, c: (0,) * len(shape))

    def tiled(*shape):
        return pl.BlockSpec(shape, lambda i, c: (i,) + (0,) * (len(shape) - 1))

    window = jax.ShapeDtypeStruct((2 * A_PAD, 2 * width), BF16)
    edge = jax.ShapeDtypeStruct((A_PAD, 2 * width), BF16)
    resident = pl.BlockSpec(memory_space=pltpu.VMEM)
    return pl.pallas_call(
        outgoing_kernel,
        grid_spec=pltpu.PrefetchScalarGridSpec(
            num_scalar_prefetch=1,
            grid=(steps,),
            in_specs=[
                tiled(1, 1, TILE * slots),
                tiled(rows, width),
                tiled(rows, width),
                tiled(TILE * slots, block_len),
                tiled(TILE * slots, block_len),
                whole((width, width)),
                whole((width, width)),
            ],
            out_specs=[resident] * 3
            + [whole((2 * A_PAD, 2 * width))] * 2
            + [whole((A_PAD, 2 * width))] * 2,
            scratch_shapes=[
                pltpu.VMEM((2 * width, 2 * width), BF16),
                pltpu.VMEM((2 * width, 2 * width), BF16),
                pltpu.VMEM((block_len, width), BF16),
                pltpu.VMEM((3 * A_PAD, 2 * width), F32),
            ],
        ),
        out_shape=[pltpu.VMEM(packed, BF16)] * 3 + [window] * 2 + [edge] * 2,
        compiler_params=pltpu.CompilerParams(vmem_limit_bytes=24 * 2**20),
        name="outgoing",
    )(counts, relative, feats, cot, send, ret, w_first, w_second)


def incoming_kernel(
    nb_ref,
    feats_ref,
    cot_ref,
    send_ref,
    w_first_ref,
    w_second_ref,
    w_coarse_ref,
    own_right_ref,
    own_left_ref,
    near_low_ref,
    near_high_ref,
    far_low_ref,
    far_high_ref,
    first_ref,
    slope1_ref,
    slope2_ref,
    grad_feats_ref,
    grads_ref,
    w1_ref,
    w2_ref,
    dcoarse_ref,
    acc1_ref,
    acc2_ref,
):
    step = pl.program_id(0)
    block_len = send_ref.shape[1]
    slots = send_ref.shape[0] // TILE
    width = feats_ref.shape[1]

    @pl.when(step == 0)
    def _():
        w1_ref[...] = diag_pair(w_first_ref[...].T * 0.5)
        w2_ref[...] = diag_pair(w_second_ref[...].T * 0.5)
        acc1_ref[...] = jnp.zeros_like(acc1_ref)
        acc2_ref[...] = jnp.zeros_like(acc2_ref)

        def load(ref, place):
            return ref[pl.ds(place * A_PAD, A_PAD), :].astype(F32)

        total = jnp.concatenate(
            [
                load(own_left_ref, 0) + load(near_low_ref, 0) + load(far_low_ref, 0),
                load(own_left_ref, 1) + load(near_low_ref, 1) + load(near_high_ref, 0),
                load(own_right_ref, 1) + load(near_high_ref, 1) + load(far_high_ref, 0),
            ],
            axis=0,
        )
        coarse = total[:, :width].astype(BF16)
        pre = dot(coarse, w_coarse_ref[...])
        sig = jax.nn.sigmoid(pre)
        slope = sig * (1.0 + pre * (1.0 - sig))
        dpre = (total[:, width:] * slope).astype(BF16)
        dcoarse_ref[...] = dot(dpre, w_coarse_ref[...].T).astype(BF16)
        grads_ref[2 * width :, :] = dot_rows(
            coarse[A_PAD : 2 * A_PAD], dpre[A_PAD : 2 * A_PAD]
        ).astype(BF16)

    send_t = send_ref[...].T
    spread_in = dot_rows(select_slots(nb_ref), dcoarse_ref[...]).astype(BF16)
    owner = lax.broadcasted_iota(jnp.int32, spread_in.shape, 0) // slots
    acc1 = jnp.zeros(acc1_ref.shape, F32)
    acc2 = jnp.zeros(acc2_ref.shape, F32)
    for pair in range(HALF):
        rows = pl.ds(pair * block_len, block_len)
        far = pl.ds((pair + HALF) * block_len, block_len)
        place = pl.ds(pl.multiple_of((step * HALF + pair) * block_len, block_len), block_len)
        share = jnp.concatenate(
            [
                jnp.where(owner == b, spread_in.astype(F32), 0.0).astype(BF16)
                for b in (pair, pair + HALF)
            ],
            axis=1,
        )
        spread = dot(send_t, share).astype(BF16)
        cot = jnp.concatenate([cot_ref[rows, :], cot_ref[far, :]], axis=1)
        dpre2 = (cot + spread) * slope2_ref[place, :]
        acc2 += dot_rows(first_ref[place, :], dpre2)
        dfirst = dot(dpre2, w2_ref[...]).astype(BF16)
        dpre1 = dfirst * slope1_ref[place, :]
        x = jnp.concatenate([feats_ref[rows, :], feats_ref[far, :]], axis=1)
        acc1 += dot_rows(x, dpre1)
        grad = dot(dpre1, w1_ref[...]).astype(BF16)
        grad_feats_ref[rows, :] = grad[:, :width]
        grad_feats_ref[far, :] = grad[:, width:]
    acc1_ref[...] += acc1
    acc2_ref[...] += acc2

    @pl.when(step == pl.num_programs(0) - 1)
    def _():
        for place, ref in enumerate((acc1_ref, acc2_ref)):
            grads_ref[pl.ds(place * width, width), :] = (
                ref[:width, :width] + ref[width:, width:]
            ).astype(BF16)


def incoming(relative, feats, cot, send, w_first, w_second, w_coarse, windows, kept):
    points, width = feats.shape
    block_len = send.shape[1]
    slots = send.shape[0] // (points // block_len)
    steps = points // (TILE * block_len)
    rows = TILE * block_len

    def whole(shape):
        return pl.BlockSpec(shape, lambda i: (0,) * len(shape))

    def tiled(*shape):
        return pl.BlockSpec(shape, lambda i: (i,) + (0,) * (len(shape) - 1))

    resident = pl.BlockSpec(memory_space=pltpu.VMEM)
    kept = [pltpu.with_memory_space_constraint(k, pltpu.VMEM) for k in kept]
    return pl.pallas_call(
        incoming_kernel,
        grid=(steps,),
        in_specs=[
            tiled(1, 1, TILE * slots),
            tiled(rows, width),
            tiled(rows, width),
            tiled(TILE * slots, block_len),
        ]
        + [whole((width, width))] * 3
        + [whole(w.shape) for w in windows]
        + [resident] * 3,
        out_specs=[tiled(rows, width), whole((3 * width, width))],
        out_shape=[
            jax.ShapeDtypeStruct((points, width), BF16),
            jax.ShapeDtypeStruct((3 * width, width), BF16),
        ],
        scratch_shapes=[
            pltpu.VMEM((2 * width, 2 * width), BF16),
            pltpu.VMEM((2 * width, 2 * width), BF16),
            pltpu.VMEM((3 * A_PAD, width), BF16),
            pltpu.VMEM((2 * width, 2 * width), F32),
            pltpu.VMEM((2 * width, 2 * width), F32),
        ],
        compiler_params=pltpu.CompilerParams(vmem_limit_bytes=24 * 2**20),
        name="incoming",
    )(relative, feats, cot, send, w_first, w_second, w_coarse, *windows, *kept)


def shifted(value, by):
    count = lax.axis_size("pts")
    pairs = [(i, i + by) for i in range(count) if 0 <= i + by < count]
    return lax.ppermute(value, "pts", pairs)


def total(value):
    count = lax.axis_size("pts")
    flips = [1]
    bit = 1
    while 2 << bit <= count:
        flips += [1 << bit, 3 << bit]
        bit += 2
    for flip in flips:
        other = lax.ppermute(value, "pts", [(i, i ^ flip) for i in range(count)])
        value = (value.astype(F32) + other.astype(F32)).astype(BF16)
    return value


def body(
    feats,
    w_first,
    w_second,
    w_coarse,
    send_weight,
    return_weight,
    neighbours,
    nbr_count,
    point_count,
    cotangent,
):
    num_blocks, num_slots, block_len = send_weight.shape
    width = feats.shape[1]
    device = lax.axis_index("pts")
    devices = lax.axis_size("pts")
    used = jnp.arange(num_slots, dtype=jnp.int32)[None, :] < nbr_count[:, None]
    relative = neighbours - (device - 1) * A_DEV
    relative = jnp.where(used, relative + (A_PAD - A_DEV) * (relative // A_DEV), -1)
    relative = relative.reshape(num_blocks // TILE, 1, TILE * num_slots)
    send = send_weight.reshape(num_blocks * num_slots, block_len)
    ret = return_weight.reshape(num_blocks * num_slots, block_len)
    *kept, to_right, to_left, edge_right, edge_left = outgoing(
        point_count, relative, feats, cotangent, send, ret, w_first, w_second
    )
    windows = (
        to_right,
        to_left,
        shifted(to_right, 1),
        shifted(to_left, -1),
        shifted(edge_right, 2),
        shifted(edge_left, -2),
    )
    grad_feats, grads = incoming(
        relative, feats, cotangent, send, w_first, w_second, w_coarse, windows, kept
    )
    grads = total(grads).astype(F32)
    total_points = devices * num_blocks * block_len
    total_atoms = devices * A_DEV
    factor = 0.5 / math.sqrt(total_points)
    return (
        grad_feats,
        grads[:width] * factor,
        grads[width : 2 * width] * factor,
        grads[2 * width :] * (1.0 / math.sqrt(total_atoms)),
    )


def solution(mesh):
    placed = (
        P("pts", None),
        P(),
        P(),
        P(),
        P("pts", None, None),
        P("pts", None, None),
        P("pts", None),
        P("pts"),
        P("pts"),
        P("pts", None),
    )
    return jax.shard_map(
        body, mesh=mesh, in_specs=placed, out_specs=(P("pts", None), P(), P(), P()), check_vma=False
    )
```

```python
import math

import jax
import jax.numpy as jnp
from jax import lax
from jax.experimental import pallas as pl
from jax.experimental.pallas import tpu as pltpu
from jax.sharding import PartitionSpec as P

A_DEV = 40
A_PAD = 48
OUT_PAIRS, OUT_GROUP = 28, 7
IN_PAIRS = 7

BF16 = jnp.bfloat16
F32 = jnp.float32


def dot(left, right):
    return jnp.dot(left, right, preferred_element_type=F32)


def dot_rows(left, right):
    return lax.dot_general(left, right, (((0,), (0,)), ((), ())), preferred_element_type=F32)


def diag_pair(weight):
    zero = jnp.zeros_like(weight)
    return jnp.concatenate(
        [jnp.concatenate([weight, zero], axis=1), jnp.concatenate([zero, weight], axis=1)], axis=0
    )


def silu_pair(half):
    up = 1.0 + jnp.tanh(half)
    value = half * up
    return value, up + value * (2.0 - up)


def span(start, size):
    return pl.ds(pl.multiple_of(start, size), size)


def outgoing_kernel(
    first_atom,
    point_count_hbm,
    nbr_count_hbm,
    neighbours_hbm,
    feats_hbm,
    cot_hbm,
    send_hbm,
    ret_hbm,
    w_first_hbm,
    w_second_hbm,
    feats_ref,
    cot_ref,
    send_ref,
    select_ref,
    first_ref,
    slope1_ref,
    slope2_ref,
    part_out_ref,
    ret_ref,
    w_first_ref,
    w_second_ref,
    neighbours_ref,
    point_count_ref,
    nbr_count_ref,
    w1_ref,
    w2_ref,
    spot_ref,
    lane_ref,
    part_ref,
    atoms_ref,
    small_sems,
    sems,
):
    block_len = send_ref.shape[1]
    width = feats_ref.shape[1]
    slots, blocks = neighbours_ref.shape
    half_blocks = blocks // 2
    steps = half_blocks // OUT_PAIRS

    smalls = [
        pltpu.make_async_copy(src, dst, small_sems.at[place])
        for place, (src, dst) in enumerate(
            (
                (w_first_hbm, w_first_ref),
                (w_second_hbm, w_second_ref),
                (point_count_hbm, point_count_ref),
                (nbr_count_hbm, nbr_count_ref),
                (neighbours_hbm, neighbours_ref),
            )
        )
    ]

    def copies(step):
        made = []
        for side in range(2):
            block = step * OUT_PAIRS + side * half_blocks
            points = span(block * block_len, OUT_PAIRS * block_len)
            edges = span(block * slots, OUT_PAIRS * slots)
            for place, (src, dst, rows) in enumerate(
                (
                    (feats_hbm, feats_ref, points),
                    (send_hbm, send_ref, edges),
                    (ret_hbm, ret_ref, edges),
                    (cot_hbm, cot_ref, points),
                )
            ):
                made.append(
                    pltpu.make_async_copy(
                        src.at[rows, :], dst.at[rows, :], sems.at[place * 2 + side, step]
                    )
                )
        return made

    for copy in smalls:
        copy.start()
    for step in range(steps):
        for copy in copies(step):
            copy.start()
    spot_ref[...] = lax.broadcasted_iota(jnp.int32, spot_ref.shape, 0).astype(F32).astype(BF16)
    lane_ref[...] = lax.broadcasted_iota(jnp.int32, lane_ref.shape, 1).astype(F32).astype(BF16)
    part_ref[...] = jnp.zeros_like(part_ref)
    for copy in smalls:
        copy.wait()
    w1_ref[...] = diag_pair(w_first_ref[...] * 0.5)
    w2_ref[...] = diag_pair(w_second_ref[...] * 0.5)
    atoms = neighbours_ref[...] - first_atom
    for step in range(steps):
        for side in range(2):
            block = step * OUT_PAIRS + side * half_blocks
            atoms_ref[step, side] = atoms[:, block : block + OUT_PAIRS]
    column = lax.broadcasted_iota(jnp.int32, (slots, select_ref.shape[1]), 1)
    slot = lax.broadcasted_iota(jnp.int32, (slots, 1), 0)

    def work(step, carry):
        for copy in copies(step):
            copy.wait()
        messages = [[], []]
        backs = [[], []]
        for group in range(0, OUT_PAIRS, OUT_GROUP):
            pairs = [step * OUT_PAIRS + group + i for i in range(OUT_GROUP)]
            near = [span(p * block_len, block_len) for p in pairs]
            far = [span((p + half_blocks) * block_len, block_len) for p in pairs]
            half1 = [
                dot(jnp.concatenate([feats_ref[n, :], feats_ref[f, :]], axis=1), w1_ref[...]).astype(
                    BF16
                )
                for n, f in zip(near, far)
            ]
            firsts = []
            for n, half in zip(near, half1):
                first, slope1 = silu_pair(half)
                first_ref[n, :] = first
                slope1_ref[n, :] = slope1
                firsts.append(first)
            half2 = [dot(first, w2_ref[...]).astype(BF16) for first in firsts]
            points = []
            counts = []
            for p, n, half in zip(pairs, near, half2):
                point, slope2 = silu_pair(half)
                count = [
                    jnp.full((slots, width), point_count_ref[b].astype(F32)).astype(BF16)
                    for b in (p, p + half_blocks)
                ]
                mask = [
                    jnp.clip(jnp.tile(c, (block_len // slots, 1)) - spot_ref[...], 0, 1) for c in count
                ]
                slope2_ref[n, :] = slope2 * jnp.concatenate(mask, axis=1)
                points.append(point)
                counts.append(count)
            for p, n, f, point, count in zip(pairs, near, far, points, counts):
                masks = [jnp.clip(jnp.concatenate([c, c], axis=1) - lane_ref[...], 0, 1) for c in count]
                edges = [span(b * slots, slots) for b in (p, p + half_blocks)]
                send = jnp.concatenate([send_ref[e, :] * m for e, m in zip(edges, masks)], axis=0)
                ret = jnp.concatenate([ret_ref[e, :] * m for e, m in zip(edges, masks)], axis=0)
                cot = jnp.concatenate([cot_ref[n, :], cot_ref[f, :]], axis=1)
                message = dot(send, point)
                back = dot(ret, cot)
                messages[0].append(message[:slots, :width])
                messages[1].append(message[slots:, width:])
                backs[0].append(back[:slots, :width])
                backs[1].append(back[slots:, width:])
        for side in range(2):
            both = jnp.concatenate(
                [jnp.concatenate(messages[side], axis=0), jnp.concatenate(backs[side], axis=0)], axis=1
            ).astype(BF16)
            block = step * OUT_PAIRS + side * half_blocks
            select = []
            for i in range(OUT_PAIRS):
                mine = jnp.where(slot < nbr_count_ref[block + i], atoms_ref[step, side, :, i : i + 1], -1)
                select.append(jnp.where(column == mine, 1.0, 0.0).astype(BF16))
            select = jnp.concatenate(select, axis=0)
            select_ref[span(block * slots, OUT_PAIRS * slots), :] = select
            part_ref[...] += dot_rows(select, both)
        return carry

    lax.fori_loop(0, steps, work, 0)
    part_out_ref[...] = jnp.zeros_like(part_out_ref)
    for place in range(3):
        part_out_ref[pl.ds(place * A_PAD, A_DEV), :] = part_ref[
            pl.ds(place * A_DEV, A_DEV), :
        ].astype(BF16)


def outgoing(
    first_atom, feats, cot, send, ret, neighbours, nbr_count, point_count, w_first, w_second
):
    points, width = feats.shape
    slots, blocks = neighbours.shape
    block_len = points // blocks
    steps = blocks // 2 // OUT_PAIRS
    packed = (points // 2, 2 * width)
    window = (3 * A_PAD, 2 * width)
    vmem = pl.BlockSpec(memory_space=pltpu.VMEM)
    hbm = pl.BlockSpec(memory_space=pltpu.HBM)
    inputs = (point_count, nbr_count, neighbours, feats, cot, send, ret, w_first, w_second)
    weight = pltpu.VMEM((width, width), BF16)
    weights = pltpu.VMEM((2 * width, 2 * width), BF16)

    def kernel(*refs):
        outgoing_kernel(first_atom(), *refs)

    return pl.pallas_call(
        kernel,
        in_specs=[hbm] * len(inputs),
        out_specs=[vmem] * 8,
        out_shape=[
            pltpu.VMEM(feats.shape, BF16),
            pltpu.VMEM(feats.shape, BF16),
            pltpu.VMEM(send.shape, BF16),
            pltpu.VMEM((blocks * slots, width), BF16),
            pltpu.VMEM(packed, BF16),
            pltpu.VMEM(packed, BF16),
            pltpu.VMEM(packed, BF16),
            pltpu.VMEM(window, BF16),
        ],
        scratch_shapes=[
            pltpu.VMEM(ret.shape, BF16),
            weight,
            weight,
            pltpu.VMEM(neighbours.shape, jnp.int32),
            pltpu.SMEM(point_count.shape, jnp.int32),
            pltpu.SMEM(nbr_count.shape, jnp.int32),
            weights,
            weights,
            pltpu.VMEM((block_len, width), BF16),
            pltpu.VMEM((slots, block_len), BF16),
            pltpu.VMEM((width, 2 * width), F32),
            pltpu.VMEM((steps, 2, slots, OUT_PAIRS), jnp.int32),
            pltpu.SemaphoreType.DMA((5,)),
            pltpu.SemaphoreType.DMA((8, steps)),
        ],
        compiler_params=pltpu.CompilerParams(vmem_limit_bytes=12 * 2**20),
        name="outgoing",
    )(*(pltpu.with_memory_space_constraint(value, pltpu.HBM) for value in inputs))


def incoming_kernel(
    side,
    w_first_ref,
    w_second_ref,
    w_coarse_ref,
    kept_ref,
    last_ref,
    feats_ref,
    cot_ref,
    send_ref,
    select_ref,
    first_ref,
    slope1_ref,
    slope2_ref,
    grad_feats_hbm,
    grads_ref,
    stage_ref,
    w1_ref,
    w2_ref,
    total_ref,
    dcoarse_ref,
    dpre1_ref,
    dpre2_ref,
    acc1_ref,
    acc2_ref,
    sems,
):
    width = feats_ref.shape[1]
    block_len = send_ref.shape[1]
    blocks = feats_ref.shape[0] // block_len
    slots = send_ref.shape[0] // blocks
    half_blocks = blocks // 2
    steps = half_blocks // IN_PAIRS
    rows = IN_PAIRS * block_len

    w1_ref[...] = diag_pair(w_first_ref[...].T * 0.5)
    w2_ref[...] = diag_pair(w_second_ref[...].T * 0.5)
    acc1_ref[...] = jnp.zeros_like(acc1_ref)
    acc2_ref[...] = jnp.zeros_like(acc2_ref)
    total_ref[span(side * A_PAD, A_PAD), :] = kept_ref[:A_PAD, :].astype(F32)
    total_ref[span((side + 1) * A_PAD, A_PAD), :] = kept_ref[A_PAD:, :].astype(F32)
    total_ref[span((1 - side) * 2 * A_PAD, A_PAD), :] = last_ref[...].astype(F32)
    coarse = total_ref[:, :width].astype(BF16)
    pre = dot(coarse, w_coarse_ref[...])
    sig = jax.nn.sigmoid(pre)
    slope = sig * (1.0 + pre * (1.0 - sig))
    dpre = (total_ref[:, width:] * slope).astype(BF16)
    dcoarse = dot(dpre, w_coarse_ref[...].T)
    dcoarse = [dcoarse[place * A_PAD : place * A_PAD + A_DEV] for place in range(3)]
    dcoarse.append(jnp.zeros((dcoarse_ref.shape[0] - 3 * A_DEV, width), F32))
    dcoarse_ref[...] = jnp.concatenate(dcoarse, axis=0).astype(BF16)
    grads_ref[2 * width :, :] = dot_rows(coarse[A_PAD : 2 * A_PAD], dpre[A_PAD : 2 * A_PAD]).astype(
        BF16
    )

    def send_out(step):
        slot = lax.rem(step, 2)
        return [
            pltpu.make_async_copy(
                stage_ref.at[slot, half],
                grad_feats_hbm.at[span(step * rows + half * half_blocks * block_len, rows), :],
                sems.at[slot, half],
            )
            for half in range(2)
        ]

    def places(step):
        pairs = [step * IN_PAIRS + i for i in range(IN_PAIRS)]
        near = [span(p * block_len, block_len) for p in pairs]
        far = [span((p + half_blocks) * block_len, block_len) for p in pairs]
        held = [pl.ds(i * block_len, block_len) for i in range(IN_PAIRS)]
        return near, far, held

    def second_grad(step):
        near, far, held = places(step)
        edges = [
            span((step * IN_PAIRS + half * half_blocks) * slots, IN_PAIRS * slots) for half in range(2)
        ]
        send_t = jnp.concatenate([send_ref[e, :] for e in edges], axis=0).T
        spread_in = jnp.concatenate([dot(select_ref[e, :], dcoarse_ref[...]) for e in edges], axis=0)
        owner = lax.broadcasted_iota(jnp.int32, spread_in.shape, 0) // slots
        for p, (n, f, h) in enumerate(zip(near, far, held)):
            share = jnp.concatenate(
                [jnp.where(owner == b, spread_in, 0.0).astype(BF16) for b in (p, p + IN_PAIRS)], axis=1
            )
            spread = dot(send_t, share).astype(BF16)
            cot = jnp.concatenate([cot_ref[n, :], cot_ref[f, :]], axis=1)
            dpre2_ref[h, :] = (cot + spread) * slope2_ref[n, :]

    def first_grad(step):
        near, _, held = places(step)
        for n, h in zip(near, held):
            dfirst = dot(dpre2_ref[h, :], w2_ref[...]).astype(BF16)
            dpre1_ref[h, :] = dfirst * slope1_ref[n, :]
        packed = span(step * IN_PAIRS * block_len, IN_PAIRS * block_len)
        acc2_ref[...] += dot_rows(first_ref[packed, :], dpre2_ref[...])

    def feats_grad(step):
        near, far, held = places(step)
        slot = lax.rem(step, 2)
        for p, h in enumerate(held):
            grad = dot(dpre1_ref[h, :], w1_ref[...]).astype(BF16)
            stage_ref[slot, 0, h, :] = grad[:, :width]
            stage_ref[slot, 1, h, :] = grad[:, width:]
        feats = [jnp.concatenate([feats_ref[n, :], feats_ref[f, :]], axis=1) for n, f in zip(near, far)]
        acc1_ref[...] += dot_rows(jnp.concatenate(feats, axis=0), dpre1_ref[...])

    def depart(step):
        for copy in send_out(step):
            copy.start()

    def work(step, carry):
        @pl.when(step >= 4)
        def _():
            for copy in send_out(step - 4):
                copy.wait()

        feats_grad(step - 2)
        first_grad(step - 1)
        second_grad(step)
        depart(step - 2)
        return carry

    second_grad(0)
    first_grad(0)
    second_grad(1)
    lax.fori_loop(2, steps, work, 0)
    for step in (steps - 2, steps - 1):
        for copy in send_out(step - 2):
            copy.wait()
        feats_grad(step)
        if step < steps - 1:
            first_grad(step + 1)
        depart(step)
    for place, ref in enumerate((acc1_ref, acc2_ref)):
        grads_ref[pl.ds(place * width, width), :] = (ref[:width, :width] + ref[width:, width:]).astype(
            BF16
        )
    for step in range(steps - 2, steps):
        for copy in send_out(step):
            copy.wait()


def incoming(side, w_first, w_second, w_coarse, kept, last, resident):
    points, width = resident[0].shape
    block_len = resident[2].shape[1]
    vmem = pl.BlockSpec(memory_space=pltpu.VMEM)
    resident = [pltpu.with_memory_space_constraint(value, pltpu.VMEM) for value in resident]
    inputs = (w_first, w_second, w_coarse, kept, last, *resident)
    weights = pltpu.VMEM((2 * width, 2 * width), BF16)
    sums = pltpu.VMEM((2 * width, 2 * width), F32)
    held = pltpu.VMEM((IN_PAIRS * block_len, 2 * width), BF16)

    def kernel(*refs):
        incoming_kernel(side(), *refs)

    return pl.pallas_call(
        kernel,
        in_specs=[vmem] * len(inputs),
        out_specs=[pl.BlockSpec(memory_space=pltpu.HBM), vmem],
        out_shape=[pltpu.HBM((points, width), BF16), jax.ShapeDtypeStruct((3 * width, width), BF16)],
        scratch_shapes=[
            pltpu.VMEM((2, 2, IN_PAIRS * block_len, width), BF16),
            weights,
            weights,
            pltpu.VMEM((3 * A_PAD, 2 * width), F32),
            pltpu.VMEM((width, width), BF16),
            held,
            held,
            sums,
            sums,
            pltpu.SemaphoreType.DMA((2, 2)),
        ],
        compiler_params=pltpu.CompilerParams(vmem_limit_bytes=12 * 2**20),
        name="incoming",
    )(*inputs)


def flipped(value, flip):
    count = lax.axis_size("pts")
    return lax.ppermute(value, "pts", [(i, i ^ flip) for i in range(count)])


def added(*values):
    total = values[0].astype(F32)
    for value in values[1:]:
        total = total + value.astype(F32)
    return total.astype(BF16)


def near_sums(part):
    count = lax.axis_size("pts")
    part = part.reshape(3, A_PAD, -1)
    odd = lax.rem(lax.axis_index("pts"), 2) == 1
    kept = jnp.where(odd, part[1:], part[:2])
    other = flipped(jnp.where(odd, part[0], part[2]), 1)
    inner = (lax.broadcasted_iota(jnp.int32, (2, 1, 1), 0) == 0) == odd
    kept = added(kept, jnp.where(inner, other[None], 0.0))
    steps = [(i, i + 1) for i in range(1, count - 1, 2)]
    kept = added(kept, lax.ppermute(kept, "pts", steps + [(j, i) for i, j in steps]))
    last = flipped(jnp.where(odd, kept[0], kept[1]), 1)
    return kept.reshape(2 * A_PAD, -1), last


def device_sum(value):
    count = lax.axis_size("pts")
    odd = lax.rem(lax.axis_index("pts"), 2) == 1
    low, high = jnp.split(value, 2, axis=0)
    part = added(jnp.where(odd, high, low), flipped(jnp.where(odd, low, high), 1))
    place = 1
    while 2 << place <= count:
        part = added(part, *(flipped(part, k << place) for k in (1, 3, 2)))
        place += 2
    other = flipped(part, 1)
    return jnp.concatenate([jnp.where(odd, other, part), jnp.where(odd, part, other)], axis=0)


def body(
    feats,
    w_first,
    w_second,
    w_coarse,
    send_weight,
    return_weight,
    neighbours,
    nbr_count,
    point_count,
    cotangent,
):
    num_blocks, num_slots, block_len = send_weight.shape
    width = feats.shape[1]
    devices = lax.axis_size("pts")
    send = send_weight.reshape(num_blocks * num_slots, block_len)
    ret = return_weight.reshape(num_blocks * num_slots, block_len)
    *resident, part = outgoing(
        lambda: (lax.axis_index("pts") - 1) * A_DEV,
        feats,
        cotangent,
        send,
        ret,
        neighbours.T,
        nbr_count,
        point_count,
        w_first,
        w_second,
    )
    kept, last = near_sums(part)
    grad_feats, grads = incoming(
        lambda: lax.rem(lax.axis_index("pts"), 2), w_first, w_second, w_coarse, kept, last, resident
    )
    grads = device_sum(grads).astype(F32)
    total_points = devices * num_blocks * block_len
    total_atoms = devices * A_DEV
    factor = 0.5 / math.sqrt(total_points)
    return (
        grad_feats,
        grads[:width] * factor,
        grads[width : 2 * width] * factor,
        grads[2 * width :] * (1.0 / math.sqrt(total_atoms)),
    )


def solution(mesh):
    placed = (
        P("pts", None),
        P(),
        P(),
        P(),
        P("pts", None, None),
        P("pts", None, None),
        P("pts", None),
        P("pts"),
        P("pts"),
        P("pts", None),
    )
    return jax.shard_map(
        body, mesh=mesh, in_specs=placed, out_specs=(P("pts", None), P(), P(), P()), check_vma=False
    )
```

```python
import math

import jax
import jax.numpy as jnp
from jax import lax
from jax.experimental import pallas as pl
from jax.experimental.pallas import tpu as pltpu
from jax.sharding import PartitionSpec as P

A_DEV = 40
A_PAD = 48
AHEAD = 2
OUT_PAIRS, OUT_MERGE = 8, 2
IN_PAIRS, IN_MERGE = 8, 2

BF16 = jnp.bfloat16
F32 = jnp.float32


def dot(left, right):
    return jnp.dot(left, right, preferred_element_type=F32)


def dot_rows(left, right):
    return lax.dot_general(left, right, (((0,), (0,)), ((), ())), preferred_element_type=F32)


def diag_pair(weight):
    zero = jnp.zeros_like(weight)
    return jnp.concatenate(
        [jnp.concatenate([weight, zero], axis=1), jnp.concatenate([zero, weight], axis=1)], axis=0
    )


def silu_pair(half):
    up = 1.0 + jnp.tanh(half)
    value = half * up
    return value, up + value * (2.0 - up)


def span(start, size):
    return pl.ds(pl.multiple_of(start, size), size)


def outgoing_kernel(
    first_atom,
    point_count_hbm,
    nbr_count_hbm,
    neighbours_hbm,
    feats_hbm,
    cot_hbm,
    send_hbm,
    ret_hbm,
    w_first_hbm,
    w_second_hbm,
    feats_ref,
    cot_ref,
    send_ref,
    select_ref,
    first_ref,
    slope1_ref,
    slope2_ref,
    part_out_ref,
    ret_ref,
    w_first_ref,
    w_second_ref,
    neighbours_ref,
    point_count_ref,
    nbr_count_ref,
    w1_ref,
    w2_ref,
    spot_ref,
    lane_ref,
    part_ref,
    atoms_ref,
    half1_ref,
    half2_ref,
    both_ref,
    small_sems,
    sems,
):
    block_len = send_ref.shape[1]
    width = feats_ref.shape[1]
    slots, blocks = neighbours_ref.shape
    half_blocks = blocks // 2
    steps = half_blocks // OUT_PAIRS

    smalls = [
        pltpu.make_async_copy(src, dst, small_sems.at[place])
        for place, (src, dst) in enumerate(
            (
                (w_first_hbm, w_first_ref),
                (w_second_hbm, w_second_ref),
                (point_count_hbm, point_count_ref),
                (nbr_count_hbm, nbr_count_ref),
                (neighbours_hbm, neighbours_ref),
            )
        )
    ]

    def copies(step, arrays):
        made = []
        for side in range(2):
            block = step * OUT_PAIRS + side * half_blocks
            points = span(block * block_len, OUT_PAIRS * block_len)
            edges = span(block * slots, OUT_PAIRS * slots)
            for place, (src, dst, rows) in enumerate(
                (
                    (feats_hbm, feats_ref, points),
                    (send_hbm, send_ref, edges),
                    (ret_hbm, ret_ref, edges),
                    (cot_hbm, cot_ref, points),
                )
            ):
                if place in arrays:
                    made.append(
                        pltpu.make_async_copy(
                            src.at[rows, :], dst.at[rows, :], sems.at[place * 2 + side, step]
                        )
                    )
        return made

    def ask(step, arrays):
        def start():
            for copy in copies(step, arrays):
                copy.start()

        if isinstance(step, int):
            if step < steps:
                start()
        else:
            pl.when(step < steps)(start)

    def arrive(step, arrays):
        for copy in copies(step, arrays):
            copy.wait()

    points_in, others_in = (0,), (1, 2, 3)
    for copy in smalls:
        copy.start()
    for step in range(AHEAD):
        ask(step, points_in)
    ask(0, others_in)
    spot_ref[...] = lax.broadcasted_iota(jnp.int32, spot_ref.shape, 0).astype(F32).astype(BF16)
    lane_ref[...] = lax.broadcasted_iota(jnp.int32, lane_ref.shape, 1).astype(F32).astype(BF16)
    part_ref[...] = jnp.zeros_like(part_ref)
    for copy in smalls:
        copy.wait()
    w1_ref[...] = diag_pair(w_first_ref[...] * 0.5)
    w2_ref[...] = diag_pair(w_second_ref[...] * 0.5)
    atoms = neighbours_ref[...] - first_atom
    for step in range(steps):
        for side in range(2):
            block = step * OUT_PAIRS + side * half_blocks
            atoms_ref[step, side] = atoms[:, block : block + OUT_PAIRS]
    column = lax.broadcasted_iota(jnp.int32, (slots, select_ref.shape[1]), 1)
    slot = lax.broadcasted_iota(jnp.int32, (slots, 1), 0)

    size = OUT_MERGE * block_len

    def rows(step, i, merge=OUT_MERGE):
        near, far = [
            pl.ds(pl.multiple_of((step * OUT_PAIRS + i + b) * block_len, block_len), merge * block_len)
            for b in (0, half_blocks)
        ]
        return near, far, pl.ds(i * block_len, merge * block_len)

    def start_layer(step, i):
        near, far, held = rows(step, i)
        x = jnp.concatenate([feats_ref[near, :], feats_ref[far, :]], axis=1)
        half1_ref[held, :] = dot(x, w1_ref[...]).astype(BF16)

    def second_layer(step, i):
        near, _, held = rows(step, i)
        first, slope1 = silu_pair(half1_ref[held, :])
        first_ref[near, :] = first
        slope1_ref[near, :] = slope1
        half2_ref[held, :] = dot(first, w2_ref[...]).astype(BF16)

    def messages(step, i):
        for j in range(i, i + OUT_MERGE):
            p = step * OUT_PAIRS + j
            near, far, held = rows(step, j, 1)
            point, slope2 = silu_pair(half2_ref[held, :])
            count = [
                jnp.full((slots, width), point_count_ref[b].astype(F32)).astype(BF16)
                for b in (p, p + half_blocks)
            ]
            mask = [jnp.clip(jnp.tile(c, (block_len // slots, 1)) - spot_ref[...], 0, 1) for c in count]
            slope2_ref[near, :] = slope2 * jnp.concatenate(mask, axis=1)
            masks = [jnp.clip(jnp.concatenate([c, c], axis=1) - lane_ref[...], 0, 1) for c in count]
            edges = [span(b * slots, slots) for b in (p, p + half_blocks)]
            send = jnp.concatenate([send_ref[e, :] * m for e, m in zip(edges, masks)], axis=0)
            ret = jnp.concatenate([ret_ref[e, :] * m for e, m in zip(edges, masks)], axis=0)
            cot = jnp.concatenate([cot_ref[near, :], cot_ref[far, :]], axis=1)
            sent = dot(send, point)
            returned = dot(ret, cot)
            mine = pl.ds(j * slots, slots)
            for side in range(2):
                lanes = slice(side * width, (side + 1) * width)
                both_ref[side, mine, :width] = sent[side * slots : (side + 1) * slots, lanes].astype(BF16)
                both_ref[side, mine, width:] = returned[side * slots : (side + 1) * slots, lanes].astype(BF16)

    def collect(step):
        for side in range(2):
            block = step * OUT_PAIRS + side * half_blocks
            select = []
            for i in range(OUT_PAIRS):
                mine = jnp.where(slot < nbr_count_ref[block + i], atoms_ref[step, side, :, i : i + 1], -1)
                select.append(jnp.where(column == mine, 1.0, 0.0).astype(BF16))
            select = jnp.concatenate(select, axis=0)
            select_ref[span(block * slots, OUT_PAIRS * slots), :] = select
            part_ref[...] += dot_rows(select, both_ref[side])

    def stages(fourth, third, second, first):
        if fourth is not None:
            collect(fourth)
        for i in range(0, OUT_PAIRS, OUT_MERGE):
            if third is not None:
                messages(third, i)
            if second is not None:
                second_layer(second, i)
            if first is not None:
                start_layer(first, i)

    def work(step, carry):
        arrive(step, points_in)
        ask(step + AHEAD, points_in)
        ask(step + 1, others_in)
        arrive(step - 2, others_in)
        stages(step - 3, step - 2, step - 1, step)
        return carry

    arrive(0, points_in)
    ask(AHEAD, points_in)
    ask(1, others_in)
    stages(None, None, None, 0)
    arrive(1, points_in)
    ask(1 + AHEAD, points_in)
    ask(2, others_in)
    stages(None, None, 0, 1)
    arrive(2, points_in)
    ask(2 + AHEAD, points_in)
    ask(3, others_in)
    arrive(0, others_in)
    stages(None, 0, 1, 2)
    lax.fori_loop(3, steps, work, 0)
    arrive(steps - 2, others_in)
    stages(steps - 3, steps - 2, steps - 1, None)
    arrive(steps - 1, others_in)
    stages(steps - 2, steps - 1, None, None)
    stages(steps - 1, None, None, None)
    part_out_ref[...] = jnp.zeros_like(part_out_ref)
    for place in range(3):
        part_out_ref[pl.ds(place * A_PAD, A_DEV), :] = part_ref[
            pl.ds(place * A_DEV, A_DEV), :
        ].astype(BF16)


def outgoing(
    first_atom, feats, cot, send, ret, neighbours, nbr_count, point_count, w_first, w_second
):
    points, width = feats.shape
    slots, blocks = neighbours.shape
    block_len = points // blocks
    steps = blocks // 2 // OUT_PAIRS
    packed = (points // 2, 2 * width)
    window = (3 * A_PAD, 2 * width)
    vmem = pl.BlockSpec(memory_space=pltpu.VMEM)
    hbm = pl.BlockSpec(memory_space=pltpu.HBM)
    inputs = (point_count, nbr_count, neighbours, feats, cot, send, ret, w_first, w_second)
    weight = pltpu.VMEM((width, width), BF16)
    weights = pltpu.VMEM((2 * width, 2 * width), BF16)

    def kernel(*refs):
        outgoing_kernel(first_atom(), *refs)

    return pl.pallas_call(
        kernel,
        in_specs=[hbm] * len(inputs),
        out_specs=[vmem] * 8,
        out_shape=[
            pltpu.VMEM(feats.shape, BF16),
            pltpu.VMEM(feats.shape, BF16),
            pltpu.VMEM(send.shape, BF16),
            pltpu.VMEM((blocks * slots, width), BF16),
            pltpu.VMEM(packed, BF16),
            pltpu.VMEM(packed, BF16),
            pltpu.VMEM(packed, BF16),
            pltpu.VMEM(window, BF16),
        ],
        scratch_shapes=[
            pltpu.VMEM(ret.shape, BF16),
            weight,
            weight,
            pltpu.VMEM(neighbours.shape, jnp.int32),
            pltpu.SMEM(point_count.shape, jnp.int32),
            pltpu.SMEM(nbr_count.shape, jnp.int32),
            weights,
            weights,
            pltpu.VMEM((block_len, width), BF16),
            pltpu.VMEM((slots, block_len), BF16),
            pltpu.VMEM((width, 2 * width), F32),
            pltpu.VMEM((steps, 2, slots, OUT_PAIRS), jnp.int32),
            pltpu.VMEM((OUT_PAIRS * block_len, 2 * width), BF16),
            pltpu.VMEM((OUT_PAIRS * block_len, 2 * width), BF16),
            pltpu.VMEM((2, OUT_PAIRS * slots, 2 * width), BF16),
            pltpu.SemaphoreType.DMA((5,)),
            pltpu.SemaphoreType.DMA((8, blocks // 2 // OUT_PAIRS)),
        ],
        compiler_params=pltpu.CompilerParams(vmem_limit_bytes=12 * 2**20),
        name="outgoing",
    )(*(pltpu.with_memory_space_constraint(value, pltpu.HBM) for value in inputs))


def incoming_kernel(
    side,
    w_first_ref,
    w_second_ref,
    w_coarse_ref,
    kept_ref,
    last_ref,
    feats_ref,
    cot_ref,
    send_ref,
    select_ref,
    first_ref,
    slope1_ref,
    slope2_ref,
    grad_feats_hbm,
    grads_ref,
    stage_ref,
    w1_ref,
    w2_ref,
    total_ref,
    send_t_ref,
    owner_ref,
    spread_in_ref,
    held1_ref,
    dpre2_ref,
    acc1_ref,
    acc2_ref,
    sems,
):
    width = feats_ref.shape[1]
    block_len = send_ref.shape[1]
    blocks = feats_ref.shape[0] // block_len
    slots = send_ref.shape[0] // blocks
    half_blocks = blocks // 2
    steps = half_blocks // IN_PAIRS

    w1_ref[...] = diag_pair(w_first_ref[...].T * 0.5)
    w2_ref[...] = diag_pair(w_second_ref[...].T * 0.5)
    acc1_ref[...] = jnp.zeros_like(acc1_ref)
    acc2_ref[...] = jnp.zeros_like(acc2_ref)
    total_ref[span(side * A_PAD, A_PAD), :] = kept_ref[:A_PAD, :].astype(F32)
    total_ref[span((side + 1) * A_PAD, A_PAD), :] = kept_ref[A_PAD:, :].astype(F32)
    total_ref[span((1 - side) * 2 * A_PAD, A_PAD), :] = last_ref[...].astype(F32)
    coarse = total_ref[:, :width].astype(BF16)
    pre = dot(coarse, w_coarse_ref[...])
    sig = jax.nn.sigmoid(pre)
    slope = sig * (1.0 + pre * (1.0 - sig))
    dpre = (total_ref[:, width:] * slope).astype(BF16)
    edge_rows = IN_PAIRS * slots
    for chunk in range(2 * steps):
        send_t_ref[chunk] = send_ref[pl.ds(chunk * edge_rows, edge_rows), :].T
    owner = lax.broadcasted_iota(jnp.int32, (edge_rows, width), 0) // slots
    for place in range(IN_PAIRS):
        owner_ref[place] = jnp.where(owner == place, 1.0, 0.0).astype(BF16)
    dcoarse = dot(dpre, w_coarse_ref[...].T)
    dcoarse = [dcoarse[place * A_PAD : place * A_PAD + A_DEV] for place in range(3)]
    dcoarse.append(jnp.zeros((select_ref.shape[1] - 3 * A_DEV, width), F32))
    dcoarse = jnp.concatenate(dcoarse, axis=0).astype(BF16)
    spread_in_ref[...] = dot(select_ref[...], dcoarse).astype(BF16)
    grads_ref[2 * width :, :] = dot_rows(coarse[A_PAD : 2 * A_PAD], dpre[A_PAD : 2 * A_PAD]).astype(
        BF16
    )

    def rows(step, i, merge=IN_MERGE):
        near, far = [
            pl.ds(pl.multiple_of((step * IN_PAIRS + i + b) * block_len, block_len), merge * block_len)
            for b in (0, half_blocks)
        ]
        return near, far, pl.ds(i * block_len, merge * block_len)

    def second_grad(step, i):
        edges = [
            span((step * IN_PAIRS + half * half_blocks) * slots, IN_PAIRS * slots) for half in range(2)
        ]
        send_t = jnp.concatenate(
            [send_t_ref[step], send_t_ref[step + half_blocks // IN_PAIRS]], axis=1
        )
        for p in range(i, i + IN_MERGE):
            near, far, held = rows(step, p, 1)
            mine = [spread_in_ref[e, :] * owner_ref[p] for e in edges]
            zero = jnp.zeros_like(mine[0])
            share = jnp.concatenate(
                [jnp.concatenate([mine[0], zero], axis=1), jnp.concatenate([zero, mine[1]], axis=1)], axis=0
            )
            spread = dot(send_t, share).astype(BF16)
            cot = jnp.concatenate([cot_ref[near, :], cot_ref[far, :]], axis=1)
            dpre2_ref[held, :] = (cot + spread) * slope2_ref[near, :]

    def first_grad(step, i):
        near, _, held = rows(step, i)
        dpre2 = dpre2_ref[held, :]
        dpre1 = dot(dpre2, w2_ref[...]).astype(BF16) * slope1_ref[near, :]
        held1_ref[held, :] = dpre1
        acc2_ref[...] += dot_rows(first_ref[near, :], dpre2)

    def send_out(step):
        slot = lax.rem(step, 2)
        size = IN_PAIRS * block_len
        return [
            pltpu.make_async_copy(
                stage_ref.at[slot, half],
                grad_feats_hbm.at[span(step * size + half * half_blocks * block_len, size), :],
                sems.at[slot, half],
            )
            for half in range(2)
        ]

    def feats_grad(step, i):
        near, far, held = rows(step, i)
        grad = dot(held1_ref[held, :], w1_ref[...]).astype(BF16)
        slot = lax.rem(step, 2)
        stage_ref[slot, 0, held, :] = grad[:, :width]
        stage_ref[slot, 1, held, :] = grad[:, width:]
        feats = jnp.concatenate([feats_ref[near, :], feats_ref[far, :]], axis=1)
        acc1_ref[...] += dot_rows(feats, held1_ref[held, :])

    def stages(third, second, first):
        for i in range(0, IN_PAIRS, IN_MERGE):
            if third is not None:
                feats_grad(third, i)
            if second is not None:
                first_grad(second, i)
            if first is not None:
                second_grad(first, i)

    def await_slot(step):
        for copy in send_out(step):
            copy.wait()

    def depart(step):
        for copy in send_out(step):
            copy.start()

    def work(step, carry):
        pl.when(step >= 4)(lambda: await_slot(step - 4))
        stages(step - 2, step - 1, step)
        depart(step - 2)
        return carry

    stages(None, None, 0)
    stages(None, 0, 1)
    lax.fori_loop(2, steps, work, 0)
    await_slot(steps - 4)
    stages(steps - 2, steps - 1, None)
    depart(steps - 2)
    await_slot(steps - 3)
    stages(steps - 1, None, None)
    depart(steps - 1)
    for place, ref in enumerate((acc1_ref, acc2_ref)):
        grads_ref[pl.ds(place * width, width), :] = (ref[:width, :width] + ref[width:, width:]).astype(
            BF16
        )
    await_slot(steps - 2)
    await_slot(steps - 1)


def incoming(side, w_first, w_second, w_coarse, kept, last, resident):
    points, width = resident[0].shape
    block_len = resident[2].shape[1]
    vmem = pl.BlockSpec(memory_space=pltpu.VMEM)
    resident = [pltpu.with_memory_space_constraint(value, pltpu.VMEM) for value in resident]
    inputs = (w_first, w_second, w_coarse, kept, last, *resident)
    weights = pltpu.VMEM((2 * width, 2 * width), BF16)
    sums = pltpu.VMEM((2 * width, 2 * width), F32)
    held = pltpu.VMEM((IN_PAIRS * block_len, 2 * width), BF16)
    edge_rows = IN_PAIRS * (resident[2].shape[0] * block_len // points)

    def kernel(*refs):
        incoming_kernel(side(), *refs)

    return pl.pallas_call(
        kernel,
        in_specs=[vmem] * len(inputs),
        out_specs=[pl.BlockSpec(memory_space=pltpu.HBM), vmem],
        out_shape=[pltpu.HBM((points, width), BF16), pltpu.VMEM((3 * width, width), BF16)],
        scratch_shapes=[
            pltpu.VMEM((2, 2, IN_PAIRS * block_len, width), BF16),
            weights,
            weights,
            pltpu.VMEM((3 * A_PAD, 2 * width), F32),
            pltpu.VMEM((resident[2].shape[0] // edge_rows, block_len, edge_rows), BF16),
            pltpu.VMEM((IN_PAIRS, edge_rows, width), BF16),
            pltpu.VMEM((resident[2].shape[0], width), BF16),
            held,
            held,
            sums,
            sums,
            pltpu.SemaphoreType.DMA((2, 2)),
        ],
        compiler_params=pltpu.CompilerParams(vmem_limit_bytes=12 * 2**20),
        name="incoming",
    )(*inputs)


def flipped(value, flip):
    count = lax.axis_size("pts")
    return lax.ppermute(value, "pts", [(i, i ^ flip) for i in range(count)])


def added(*values):
    total = values[0].astype(F32)
    for value in values[1:]:
        total = total + value.astype(F32)
    return total.astype(BF16)


def near_sums(part):
    count = lax.axis_size("pts")
    part = part.reshape(3, A_PAD, -1)
    odd = lax.rem(lax.axis_index("pts"), 2) == 1
    kept = jnp.where(odd, part[1:], part[:2])
    other = flipped(jnp.where(odd, part[0], part[2]), 1)
    inner = (lax.broadcasted_iota(jnp.int32, (2, 1, 1), 0) == 0) == odd
    kept = added(kept, jnp.where(inner, other[None], 0.0))
    steps = [(i, i + 1) for i in range(1, count - 1, 2)]
    kept = added(kept, lax.ppermute(kept, "pts", steps + [(j, i) for i, j in steps]))
    last = flipped(jnp.where(odd, kept[0], kept[1]), 1)
    return kept.reshape(2 * A_PAD, -1), last


def device_sum(value):
    count = lax.axis_size("pts")
    odd = lax.rem(lax.axis_index("pts"), 2) == 1
    low, high = jnp.split(value, 2, axis=0)
    part = added(jnp.where(odd, high, low), flipped(jnp.where(odd, low, high), 1))
    place = 1
    while 2 << place <= count:
        part = added(part, *(flipped(part, k << place) for k in (1, 3, 2)))
        place += 2
    other = flipped(part, 1)
    return jnp.concatenate([jnp.where(odd, other, part), jnp.where(odd, part, other)], axis=0)


def body(
    feats,
    w_first,
    w_second,
    w_coarse,
    send_weight,
    return_weight,
    neighbours,
    nbr_count,
    point_count,
    cotangent,
):
    num_blocks, num_slots, block_len = send_weight.shape
    width = feats.shape[1]
    devices = lax.axis_size("pts")
    send = send_weight.reshape(num_blocks * num_slots, block_len)
    ret = return_weight.reshape(num_blocks * num_slots, block_len)
    *resident, part = outgoing(
        lambda: (lax.axis_index("pts") - 1) * A_DEV,
        feats,
        cotangent,
        send,
        ret,
        neighbours.T,
        nbr_count,
        point_count,
        w_first,
        w_second,
    )
    kept, last = near_sums(part)
    grad_feats, grads = incoming(
        lambda: lax.rem(lax.axis_index("pts"), 2), w_first, w_second, w_coarse, kept, last, resident
    )
    grads = device_sum(grads).astype(F32)
    total_points = devices * num_blocks * block_len
    total_atoms = devices * A_DEV
    factor = 0.5 / math.sqrt(total_points)
    return (
        grad_feats,
        grads[:width] * factor,
        grads[width : 2 * width] * factor,
        grads[2 * width :] * (1.0 / math.sqrt(total_atoms)),
    )


def solution(mesh):
    placed = (
        P("pts", None),
        P(),
        P(),
        P(),
        P("pts", None, None),
        P("pts", None, None),
        P("pts", None),
        P("pts"),
        P("pts"),
        P("pts", None),
    )
    return jax.shard_map(
        body, mesh=mesh, in_specs=placed, out_specs=(P("pts", None), P(), P(), P()), check_vma=False
    )
```

```python
import functools
import math

import jax
import jax.numpy as jnp
from jax import lax
from jax.experimental import pallas as pl
from jax.experimental.pallas import tpu as pltpu
from jax.sharding import PartitionSpec as P

A_DEV = 40
A_PAD = 48
AHEAD = 2
OUT_PAIRS, OUT_MERGE = 8, 2
IN_PAIRS, IN_MERGE = 8, 2
FEATS_PARTS = (20, 18, 18)
FEATS_GROUP = 4

BF16 = jnp.bfloat16
F32 = jnp.float32


def dot(left, right):
    return jnp.dot(left, right, preferred_element_type=F32)


def dot_rows(left, right):
    return lax.dot_general(left, right, (((0,), (0,)), ((), ())), preferred_element_type=F32)


def diag_pair(weight):
    zero = jnp.zeros_like(weight)
    return jnp.concatenate(
        [jnp.concatenate([weight, zero], axis=1), jnp.concatenate([zero, weight], axis=1)], axis=0
    )


def silu_pair(half):
    up = 1.0 + jnp.tanh(half)
    value = half * up
    return value, up + value * (2.0 - up)


def span(start, size):
    return pl.ds(pl.multiple_of(start, size), size)


def outgoing_kernel(
    first_atom,
    point_count_hbm,
    nbr_count_hbm,
    neighbours_hbm,
    feats_hbm,
    cot_hbm,
    send_hbm,
    ret_hbm,
    w_first_hbm,
    w_second_hbm,
    feats_ref,
    cot_ref,
    send_ref,
    select_ref,
    first_ref,
    slope1_ref,
    slope2_ref,
    part_out_ref,
    ret_ref,
    w_first_ref,
    w_second_ref,
    neighbours_ref,
    point_count_ref,
    nbr_count_ref,
    w1_ref,
    w2_ref,
    spot_ref,
    lane_ref,
    part_ref,
    atoms_ref,
    half1_ref,
    half2_ref,
    both_ref,
    small_sems,
    sems,
):
    block_len = send_ref.shape[1]
    width = feats_ref.shape[1]
    slots, blocks = neighbours_ref.shape
    half_blocks = blocks // 2
    steps = half_blocks // OUT_PAIRS

    smalls = [
        pltpu.make_async_copy(src, dst, small_sems.at[place])
        for place, (src, dst) in enumerate(
            (
                (w_first_hbm, w_first_ref),
                (w_second_hbm, w_second_ref),
                (point_count_hbm, point_count_ref),
                (nbr_count_hbm, nbr_count_ref),
                (neighbours_hbm, neighbours_ref),
            )
        )
    ]

    def copies(step, arrays):
        made = []
        for side in range(2):
            block = step * OUT_PAIRS + side * half_blocks
            points = span(block * block_len, OUT_PAIRS * block_len)
            edges = span(block * slots, OUT_PAIRS * slots)
            for place, (src, dst, rows) in enumerate(
                (
                    (feats_hbm, feats_ref, points),
                    (send_hbm, send_ref, edges),
                    (ret_hbm, ret_ref, edges),
                    (cot_hbm, cot_ref, points),
                )
            ):
                if place in arrays:
                    made.append(
                        pltpu.make_async_copy(
                            src.at[rows, :], dst.at[rows, :], sems.at[place * 2 + side, step]
                        )
                    )
        return made

    def ask(step, arrays):
        def start():
            for copy in copies(step, arrays):
                copy.start()

        if isinstance(step, int):
            if step < steps:
                start()
        else:
            pl.when(step < steps)(start)

    def arrive(step, arrays):
        for copy in copies(step, arrays):
            copy.wait()

    points_in, others_in = (0,), (1, 2, 3)
    for copy in smalls:
        copy.start()
    for step in range(AHEAD):
        ask(step, points_in)
    ask(0, others_in)
    spot_ref[...] = lax.broadcasted_iota(jnp.int32, spot_ref.shape, 0).astype(F32).astype(BF16)
    lane_ref[...] = lax.broadcasted_iota(jnp.int32, lane_ref.shape, 1).astype(F32).astype(BF16)
    part_ref[...] = jnp.zeros_like(part_ref)
    for copy in smalls:
        copy.wait()
    w1_ref[...] = diag_pair(w_first_ref[...] * 0.5)
    w2_ref[...] = diag_pair(w_second_ref[...] * 0.5)
    atoms = neighbours_ref[...] - first_atom
    for step in range(steps):
        for side in range(2):
            block = step * OUT_PAIRS + side * half_blocks
            atoms_ref[step, side] = atoms[:, block : block + OUT_PAIRS]
    column = lax.broadcasted_iota(jnp.int32, (slots, select_ref.shape[1]), 1)
    slot = lax.broadcasted_iota(jnp.int32, (slots, 1), 0)

    size = OUT_MERGE * block_len

    def rows(step, i, merge=OUT_MERGE):
        near, far = [
            pl.ds(pl.multiple_of((step * OUT_PAIRS + i + b) * block_len, block_len), merge * block_len)
            for b in (0, half_blocks)
        ]
        return near, far, pl.ds(i * block_len, merge * block_len)

    def start_layer(step, i):
        near, far, held = rows(step, i)
        x = jnp.concatenate([feats_ref[near, :], feats_ref[far, :]], axis=1)
        half1_ref[held, :] = dot(x, w1_ref[...]).astype(BF16)

    def second_layer(step, i):
        near, _, held = rows(step, i)
        first, slope1 = silu_pair(half1_ref[held, :])
        first_ref[near, :] = first
        slope1_ref[near, :] = slope1
        half2_ref[held, :] = dot(first, w2_ref[...]).astype(BF16)

    def messages(step, i):
        for j in range(i, i + OUT_MERGE):
            p = step * OUT_PAIRS + j
            near, far, held = rows(step, j, 1)
            point, slope2 = silu_pair(half2_ref[held, :])
            count = [
                jnp.full((slots, width), point_count_ref[b].astype(F32)).astype(BF16)
                for b in (p, p + half_blocks)
            ]
            mask = [jnp.clip(jnp.tile(c, (block_len // slots, 1)) - spot_ref[...], 0, 1) for c in count]
            slope2_ref[near, :] = slope2 * jnp.concatenate(mask, axis=1)
            masks = [jnp.clip(jnp.concatenate([c, c], axis=1) - lane_ref[...], 0, 1) for c in count]
            edges = [span(b * slots, slots) for b in (p, p + half_blocks)]
            send = jnp.concatenate([send_ref[e, :] * m for e, m in zip(edges, masks)], axis=0)
            ret = jnp.concatenate([ret_ref[e, :] * m for e, m in zip(edges, masks)], axis=0)
            cot = jnp.concatenate([cot_ref[near, :], cot_ref[far, :]], axis=1)
            sent = dot(send, point)
            returned = dot(ret, cot)
            mine = pl.ds(j * slots, slots)
            for side in range(2):
                lanes = slice(side * width, (side + 1) * width)
                both_ref[side, mine, :width] = sent[side * slots : (side + 1) * slots, lanes].astype(BF16)
                both_ref[side, mine, width:] = returned[side * slots : (side + 1) * slots, lanes].astype(BF16)

    def collect(step):
        for side in range(2):
            block = step * OUT_PAIRS + side * half_blocks
            select = []
            for i in range(OUT_PAIRS):
                mine = jnp.where(slot < nbr_count_ref[block + i], atoms_ref[step, side, :, i : i + 1], -1)
                select.append(jnp.where(column == mine, 1.0, 0.0).astype(BF16))
            select = jnp.concatenate(select, axis=0)
            select_ref[span(block * slots, OUT_PAIRS * slots), :] = select
            part_ref[...] += dot_rows(select, both_ref[side])

    def stages(fourth, third, second, first):
        if fourth is not None:
            collect(fourth)
        for i in range(0, OUT_PAIRS, OUT_MERGE):
            if third is not None:
                messages(third, i)
            if second is not None:
                second_layer(second, i)
            if first is not None:
                start_layer(first, i)

    def work(step, carry):
        arrive(step, points_in)
        ask(step + AHEAD, points_in)
        ask(step + 1, others_in)
        arrive(step - 2, others_in)
        stages(step - 3, step - 2, step - 1, step)
        return carry

    arrive(0, points_in)
    ask(AHEAD, points_in)
    ask(1, others_in)
    stages(None, None, None, 0)
    arrive(1, points_in)
    ask(1 + AHEAD, points_in)
    ask(2, others_in)
    stages(None, None, 0, 1)
    arrive(2, points_in)
    ask(2 + AHEAD, points_in)
    ask(3, others_in)
    arrive(0, others_in)
    stages(None, 0, 1, 2)
    lax.fori_loop(3, steps, work, 0)
    arrive(steps - 2, others_in)
    stages(steps - 3, steps - 2, steps - 1, None)
    arrive(steps - 1, others_in)
    stages(steps - 2, steps - 1, None, None)
    stages(steps - 1, None, None, None)
    part_out_ref[...] = jnp.zeros_like(part_out_ref)
    for place in range(3):
        part_out_ref[pl.ds(place * A_PAD, A_DEV), :] = part_ref[
            pl.ds(place * A_DEV, A_DEV), :
        ].astype(BF16)


def outgoing(
    first_atom, feats, cot, send, ret, neighbours, nbr_count, point_count, w_first, w_second
):
    points, width = feats.shape
    slots, blocks = neighbours.shape
    block_len = points // blocks
    steps = blocks // 2 // OUT_PAIRS
    packed = (points // 2, 2 * width)
    window = (3 * A_PAD, 2 * width)
    vmem = pl.BlockSpec(memory_space=pltpu.VMEM)
    hbm = pl.BlockSpec(memory_space=pltpu.HBM)
    inputs = (point_count, nbr_count, neighbours, feats, cot, send, ret, w_first, w_second)
    weight = pltpu.VMEM((width, width), BF16)
    weights = pltpu.VMEM((2 * width, 2 * width), BF16)

    def kernel(*refs):
        outgoing_kernel(first_atom(), *refs)

    return pl.pallas_call(
        kernel,
        in_specs=[hbm] * len(inputs),
        out_specs=[vmem] * 8,
        out_shape=[
            pltpu.VMEM(feats.shape, BF16),
            pltpu.VMEM(feats.shape, BF16),
            pltpu.VMEM(send.shape, BF16),
            pltpu.VMEM((blocks * slots, width), BF16),
            pltpu.VMEM(packed, BF16),
            pltpu.VMEM(packed, BF16),
            pltpu.VMEM(packed, BF16),
            pltpu.VMEM(window, BF16),
        ],
        scratch_shapes=[
            pltpu.VMEM(ret.shape, BF16),
            weight,
            weight,
            pltpu.VMEM(neighbours.shape, jnp.int32),
            pltpu.SMEM(point_count.shape, jnp.int32),
            pltpu.SMEM(nbr_count.shape, jnp.int32),
            weights,
            weights,
            pltpu.VMEM((block_len, width), BF16),
            pltpu.VMEM((slots, block_len), BF16),
            pltpu.VMEM((width, 2 * width), F32),
            pltpu.VMEM((steps, 2, slots, OUT_PAIRS), jnp.int32),
            pltpu.VMEM((OUT_PAIRS * block_len, 2 * width), BF16),
            pltpu.VMEM((OUT_PAIRS * block_len, 2 * width), BF16),
            pltpu.VMEM((2, OUT_PAIRS * slots, 2 * width), BF16),
            pltpu.SemaphoreType.DMA((5,)),
            pltpu.SemaphoreType.DMA((8, blocks // 2 // OUT_PAIRS)),
        ],
        compiler_params=pltpu.CompilerParams(vmem_limit_bytes=12 * 2**20),
        name="outgoing",
    )(*(pltpu.with_memory_space_constraint(value, pltpu.HBM) for value in inputs))


def incoming_kernel(
    side,
    w_second_ref,
    w_coarse_ref,
    kept_ref,
    last_ref,
    feats_ref,
    cot_ref,
    send_ref,
    select_ref,
    first_ref,
    slope1_ref,
    slope2_ref,
    dpre1_ref,
    grads_ref,
    w2_ref,
    total_ref,
    send_t_ref,
    owner_ref,
    spread_in_ref,
    held1_ref,
    dpre2_ref,
    acc1_ref,
    acc2_ref,
):
    width = feats_ref.shape[1]
    block_len = send_ref.shape[1]
    blocks = feats_ref.shape[0] // block_len
    slots = send_ref.shape[0] // blocks
    half_blocks = blocks // 2
    steps = half_blocks // IN_PAIRS

    w2_ref[...] = diag_pair(w_second_ref[...].T * 0.5)
    acc1_ref[...] = jnp.zeros_like(acc1_ref)
    acc2_ref[...] = jnp.zeros_like(acc2_ref)
    total_ref[span(side * A_PAD, A_PAD), :] = kept_ref[:A_PAD, :].astype(F32)
    total_ref[span((side + 1) * A_PAD, A_PAD), :] = kept_ref[A_PAD:, :].astype(F32)
    total_ref[span((1 - side) * 2 * A_PAD, A_PAD), :] = last_ref[...].astype(F32)
    coarse = total_ref[:, :width].astype(BF16)
    pre = dot(coarse, w_coarse_ref[...])
    sig = jax.nn.sigmoid(pre)
    slope = sig * (1.0 + pre * (1.0 - sig))
    dpre = (total_ref[:, width:] * slope).astype(BF16)
    edge_rows = IN_PAIRS * slots
    for chunk in range(2 * steps):
        send_t_ref[chunk] = send_ref[pl.ds(chunk * edge_rows, edge_rows), :].T
    owner = lax.broadcasted_iota(jnp.int32, (edge_rows, width), 0) // slots
    for place in range(IN_PAIRS):
        owner_ref[place] = jnp.where(owner == place, 1.0, 0.0).astype(BF16)
    dcoarse = dot(dpre, w_coarse_ref[...].T)
    dcoarse = [dcoarse[place * A_PAD : place * A_PAD + A_DEV] for place in range(3)]
    dcoarse.append(jnp.zeros((select_ref.shape[1] - 3 * A_DEV, width), F32))
    dcoarse = jnp.concatenate(dcoarse, axis=0).astype(BF16)
    spread_in_ref[...] = dot(select_ref[...], dcoarse).astype(BF16)
    grads_ref[2 * width :, :] = dot_rows(coarse[A_PAD : 2 * A_PAD], dpre[A_PAD : 2 * A_PAD]).astype(
        BF16
    )

    def rows(step, i, merge=IN_MERGE):
        near, far = [
            pl.ds(pl.multiple_of((step * IN_PAIRS + i + b) * block_len, block_len), merge * block_len)
            for b in (0, half_blocks)
        ]
        return near, far, pl.ds(i * block_len, merge * block_len)

    def second_grad(step, i):
        edges = [
            span((step * IN_PAIRS + half * half_blocks) * slots, IN_PAIRS * slots) for half in range(2)
        ]
        send_t = jnp.concatenate(
            [send_t_ref[step], send_t_ref[step + half_blocks // IN_PAIRS]], axis=1
        )
        for p in range(i, i + IN_MERGE):
            near, far, held = rows(step, p, 1)
            mine = [spread_in_ref[e, :] * owner_ref[p] for e in edges]
            zero = jnp.zeros_like(mine[0])
            share = jnp.concatenate(
                [jnp.concatenate([mine[0], zero], axis=1), jnp.concatenate([zero, mine[1]], axis=1)], axis=0
            )
            spread = dot(send_t, share).astype(BF16)
            cot = jnp.concatenate([cot_ref[near, :], cot_ref[far, :]], axis=1)
            dpre2_ref[held, :] = (cot + spread) * slope2_ref[near, :]

    def first_grad(step, i):
        near, _, held = rows(step, i)
        dpre2 = dpre2_ref[held, :]
        dpre1 = dot(dpre2, w2_ref[...]).astype(BF16) * slope1_ref[near, :]
        dpre1_ref[near, :] = dpre1
        held1_ref[held, :] = dpre1
        acc2_ref[...] += dot_rows(first_ref[near, :], dpre2)

    def feats_sum(step, i):
        near, far, held = rows(step, i)
        feats = jnp.concatenate([feats_ref[near, :], feats_ref[far, :]], axis=1)
        acc1_ref[...] += dot_rows(feats, held1_ref[held, :])

    def stages(third, second, first):
        for i in range(0, IN_PAIRS, IN_MERGE):
            if third is not None:
                feats_sum(third, i)
            if second is not None:
                first_grad(second, i)
            if first is not None:
                second_grad(first, i)

    def work(step, carry):
        stages(step - 2, step - 1, step)
        return carry

    stages(None, None, 0)
    stages(None, 0, 1)
    lax.fori_loop(2, steps, work, 0)
    stages(steps - 2, steps - 1, None)
    stages(steps - 1, None, None)
    for place, ref in enumerate((acc1_ref, acc2_ref)):
        grads_ref[pl.ds(place * width, width), :] = (ref[:width, :width] + ref[width:, width:]).astype(
            BF16
        )


def incoming(side, w_second, w_coarse, kept, last, resident):
    points, width = resident[0].shape
    block_len = resident[2].shape[1]
    vmem = pl.BlockSpec(memory_space=pltpu.VMEM)
    resident = [pltpu.with_memory_space_constraint(value, pltpu.VMEM) for value in resident]
    inputs = (w_second, w_coarse, kept, last, *resident)
    weights = pltpu.VMEM((2 * width, 2 * width), BF16)
    sums = pltpu.VMEM((2 * width, 2 * width), F32)
    held = pltpu.VMEM((IN_PAIRS * block_len, 2 * width), BF16)
    edge_rows = IN_PAIRS * (resident[2].shape[0] * block_len // points)

    def kernel(*refs):
        incoming_kernel(side(), *refs)

    return pl.pallas_call(
        kernel,
        in_specs=[vmem] * len(inputs),
        out_specs=[vmem, vmem],
        out_shape=[pltpu.VMEM((points // 2, 2 * width), BF16), pltpu.VMEM((3 * width, width), BF16)],
        input_output_aliases={9: 0},
        scratch_shapes=[
            weights,
            pltpu.VMEM((3 * A_PAD, 2 * width), F32),
            pltpu.VMEM((resident[2].shape[0] // edge_rows, block_len, edge_rows), BF16),
            pltpu.VMEM((IN_PAIRS, edge_rows, width), BF16),
            pltpu.VMEM((resident[2].shape[0], width), BF16),
            held,
            held,
            sums,
            sums,
        ],
        compiler_params=pltpu.CompilerParams(vmem_limit_bytes=12 * 2**20),
        name="incoming",
    )(*inputs)


def feats_grad_kernel(first, block_len, dpre1_ref, w_first_ref, *refs):
    grad_feats_hbm, stage_ref, w1_ref, sems = refs[-4:]
    width = w_first_ref.shape[0]
    half_rows = dpre1_ref.shape[0]
    rows = stage_ref.shape[1]
    w1_ref[...] = diag_pair(w_first_ref[...].T * 0.5)
    group = FEATS_GROUP * block_len
    copies = []
    for place, start in enumerate(range(0, rows, group)):
        size = min(group, rows - start)
        grad = dot(dpre1_ref[pl.ds(first + start, size), :], w1_ref[...]).astype(BF16)
        for half in range(2):
            stage_ref[half, pl.ds(start, size), :] = grad[:, half * width : (half + 1) * width]
            copies.append(
                pltpu.make_async_copy(
                    stage_ref.at[half, pl.ds(start, size), :],
                    grad_feats_hbm.at[pl.ds(half * half_rows + first + start, size), :],
                    sems.at[half, place],
                )
            )
            copies[-1].start()
    for copy in copies:
        copy.wait()


def feats_grad(first, pairs, block_len, dpre1, w_first, grad_feats):
    width = w_first.shape[0]
    half_rows = dpre1.shape[0]
    rows = pairs * block_len
    vmem = pl.BlockSpec(memory_space=pltpu.VMEM)
    hbm = pl.BlockSpec(memory_space=pltpu.HBM)
    inputs = [pltpu.with_memory_space_constraint(dpre1, pltpu.VMEM), w_first]
    if grad_feats is not None:
        inputs.append(pltpu.with_memory_space_constraint(grad_feats, pltpu.HBM))
    return pl.pallas_call(
        functools.partial(feats_grad_kernel, first * block_len, block_len),
        in_specs=[vmem, vmem, hbm][: len(inputs)],
        out_specs=hbm,
        out_shape=pltpu.HBM((2 * half_rows, width), BF16),
        input_output_aliases={} if grad_feats is None else {2: 0},
        scratch_shapes=[
            pltpu.VMEM((2, rows, width), BF16),
            pltpu.VMEM((2 * width, 2 * width), BF16),
            pltpu.SemaphoreType.DMA((2, pl.cdiv(pairs, FEATS_GROUP))),
        ],
        compiler_params=pltpu.CompilerParams(vmem_limit_bytes=12 * 2**20),
        cost_estimate=pl.CostEstimate(
            flops=4 * rows * width * width, bytes_accessed=4 * rows * width * 2, transcendentals=0
        ),
        name="feats_grad",
    )(*inputs)


def flipped(value, flip):
    count = lax.axis_size("pts")
    return lax.ppermute(value, "pts", [(i, i ^ flip) for i in range(count)])


def turned(value, place, by):
    count = lax.axis_size("pts")
    targets = [(i & ~(3 << place)) | (((i >> place) + by & 3) << place) for i in range(count)]
    return lax.ppermute(value, "pts", list(enumerate(targets)))


def added(*values):
    total = values[0].astype(F32)
    for value in values[1:]:
        total = total + value.astype(F32)
    return total.astype(BF16)


def near_sums(part):
    count = lax.axis_size("pts")
    part = part.reshape(3, A_PAD, -1)
    odd = lax.rem(lax.axis_index("pts"), 2) == 1
    kept = jnp.where(odd, part[1:], part[:2])
    other = flipped(jnp.where(odd, part[0], part[2]), 1)
    inner = (lax.broadcasted_iota(jnp.int32, (2, 1, 1), 0) == 0) == odd
    kept = added(kept, jnp.where(inner, other[None], 0.0))
    steps = [(i, i + 1) for i in range(1, count - 1, 2)]
    kept = added(kept, lax.ppermute(kept, "pts", steps + [(j, i) for i, j in steps]))
    last = flipped(jnp.where(odd, kept[0], kept[1]), 1)
    return kept.reshape(2 * A_PAD, -1), last


def device_sum(value, beside):
    count = lax.axis_size("pts")
    odd = lax.rem(lax.axis_index("pts"), 2) == 1
    low, high = jnp.split(value, 2, axis=0)
    part = added(jnp.where(odd, high, low), flipped(jnp.where(odd, low, high), 1))
    place = 1
    while 2 << place <= count:
        part, result = beside(part)
        one, three, two = [turned(part, place, k) for k in (1, 3, 2)]
        total = (part.astype(F32) + two.astype(F32)) + (one.astype(F32) + three.astype(F32))
        part = total.astype(BF16)
        part, result = lax.optimization_barrier((part, result))
        place += 2
    other = flipped(part, 1)
    return jnp.concatenate([jnp.where(odd, other, part), jnp.where(odd, part, other)], axis=0), result


def body(
    feats,
    w_first,
    w_second,
    w_coarse,
    send_weight,
    return_weight,
    neighbours,
    nbr_count,
    point_count,
    cotangent,
):
    num_blocks, num_slots, block_len = send_weight.shape
    width = feats.shape[1]
    devices = lax.axis_size("pts")
    send = send_weight.reshape(num_blocks * num_slots, block_len)
    ret = return_weight.reshape(num_blocks * num_slots, block_len)
    *resident, part = outgoing(
        lambda: (lax.axis_index("pts") - 1) * A_DEV,
        feats,
        cotangent,
        send,
        ret,
        neighbours.T,
        nbr_count,
        point_count,
        w_first,
        w_second,
    )
    kept, last = near_sums(part)
    dpre1, grads = incoming(
        lambda: lax.rem(lax.axis_index("pts"), 2), w_second, w_coarse, kept, last, resident
    )
    grad_feats = None
    done = 0
    left = list(FEATS_PARTS)

    def beside(part):
        nonlocal grad_feats, done
        held, part = lax.optimization_barrier((dpre1, part))
        size = left.pop(0)
        grad_feats = feats_grad(done, size, block_len, held, w_first, grad_feats)
        done += size
        return part, grad_feats

    grads, grad_feats = device_sum(grads, beside)
    grads = grads.astype(F32)
    total_points = devices * num_blocks * block_len
    total_atoms = devices * A_DEV
    factor = 0.5 / math.sqrt(total_points)
    return (
        grad_feats,
        grads[:width] * factor,
        grads[width : 2 * width] * factor,
        grads[2 * width :] * (1.0 / math.sqrt(total_atoms)),
    )


def solution(mesh):
    placed = (
        P("pts", None),
        P(),
        P(),
        P(),
        P("pts", None, None),
        P("pts", None, None),
        P("pts", None),
        P("pts"),
        P("pts"),
        P("pts", None),
    )
    return jax.shard_map(
        body, mesh=mesh, in_specs=placed, out_specs=(P("pts", None), P(), P(), P()), check_vma=False
    )
```

```python
import functools
import math

import jax
import jax.numpy as jnp
from jax import lax
from jax.experimental import pallas as pl
from jax.experimental.pallas import tpu as pltpu
from jax.sharding import PartitionSpec as P

A_DEV = 40
A_PAD = 48
AHEAD = 2
OUT_PAIRS, OUT_MERGE = 8, 2
IN_PAIRS, IN_MERGE = 8, 2
FEATS_PARTS = (20, 18, 18)
FEATS_GROUP = 4

BF16 = jnp.bfloat16
F32 = jnp.float32


def dot(left, right):
    return jnp.dot(left, right, preferred_element_type=F32)


def dot_rows(left, right):
    return lax.dot_general(left, right, (((0,), (0,)), ((), ())), preferred_element_type=F32)


def diag_pair(weight):
    zero = jnp.zeros_like(weight)
    return jnp.concatenate(
        [jnp.concatenate([weight, zero], axis=1), jnp.concatenate([zero, weight], axis=1)], axis=0
    )


def silu_pair(half):
    up = 1.0 + jnp.tanh(half)
    value = half * up
    return value, up + value * (2.0 - up)


def span(start, size):
    return pl.ds(pl.multiple_of(start, size), size)


def outgoing_kernel(
    first_atom,
    point_count_hbm,
    nbr_count_hbm,
    neighbours_hbm,
    feats_hbm,
    cot_hbm,
    send_hbm,
    ret_hbm,
    w_first_hbm,
    w_second_hbm,
    feats_ref,
    cot_ref,
    send_ref,
    select_ref,
    first_ref,
    slope1_ref,
    slope2_ref,
    part_out_ref,
    ret_ref,
    w_first_ref,
    w_second_ref,
    neighbours_ref,
    point_count_ref,
    nbr_count_ref,
    w1_ref,
    w2_ref,
    spot_ref,
    lane_ref,
    part_ref,
    atoms_ref,
    half1_ref,
    half2_ref,
    both_ref,
    small_sems,
    sems,
):
    block_len = send_ref.shape[1]
    width = feats_ref.shape[1]
    slots, blocks = neighbours_ref.shape
    half_blocks = blocks // 2
    steps = half_blocks // OUT_PAIRS

    smalls = [
        pltpu.make_async_copy(src, dst, small_sems.at[place])
        for place, (src, dst) in enumerate(
            (
                (w_first_hbm, w_first_ref),
                (w_second_hbm, w_second_ref),
                (point_count_hbm, point_count_ref),
                (nbr_count_hbm, nbr_count_ref),
                (neighbours_hbm, neighbours_ref),
            )
        )
    ]

    def copies(step, arrays):
        made = []
        for side in range(2):
            block = step * OUT_PAIRS + side * half_blocks
            points = span(block * block_len, OUT_PAIRS * block_len)
            edges = span(block * slots, OUT_PAIRS * slots)
            for place, (src, dst, rows) in enumerate(
                (
                    (feats_hbm, feats_ref, points),
                    (send_hbm, send_ref, edges),
                    (ret_hbm, ret_ref, edges),
                    (cot_hbm, cot_ref, points),
                )
            ):
                if place in arrays:
                    made.append(
                        pltpu.make_async_copy(
                            src.at[rows, :], dst.at[rows, :], sems.at[place * 2 + side, step]
                        )
                    )
        return made

    def ask(step, arrays):
        def start():
            for copy in copies(step, arrays):
                copy.start()

        if isinstance(step, int):
            if step < steps:
                start()
        else:
            pl.when(step < steps)(start)

    def arrive(step, arrays):
        for copy in copies(step, arrays):
            copy.wait()

    points_in, others_in = (0,), (1, 2, 3)
    for copy in smalls:
        copy.start()
    for step in range(AHEAD):
        ask(step, points_in)
    ask(0, others_in)
    spot_ref[...] = lax.broadcasted_iota(jnp.int32, spot_ref.shape, 0).astype(F32).astype(BF16)
    lane_ref[...] = lax.broadcasted_iota(jnp.int32, lane_ref.shape, 1).astype(F32).astype(BF16)
    part_ref[...] = jnp.zeros_like(part_ref)
    for copy in smalls:
        copy.wait()
    w1_ref[...] = diag_pair(w_first_ref[...] * 0.5)
    w2_ref[...] = diag_pair(w_second_ref[...] * 0.5)
    atoms = neighbours_ref[...] - first_atom
    for step in range(steps):
        for side in range(2):
            block = step * OUT_PAIRS + side * half_blocks
            atoms_ref[step, side] = atoms[:, block : block + OUT_PAIRS]
    column = lax.broadcasted_iota(jnp.int32, (slots, select_ref.shape[1]), 1)
    slot = lax.broadcasted_iota(jnp.int32, (slots, 1), 0)

    size = OUT_MERGE * block_len

    def rows(step, i, merge=OUT_MERGE):
        near, far = [
            pl.ds(pl.multiple_of((step * OUT_PAIRS + i + b) * block_len, block_len), merge * block_len)
            for b in (0, half_blocks)
        ]
        return near, far, pl.ds(i * block_len, merge * block_len)

    def start_layer(step, i):
        near, far, held = rows(step, i)
        x = jnp.concatenate([feats_ref[near, :], feats_ref[far, :]], axis=1)
        half1_ref[held, :] = dot(x, w1_ref[...]).astype(BF16)

    def second_layer(step, i):
        near, _, held = rows(step, i)
        first, slope1 = silu_pair(half1_ref[held, :])
        first_ref[near, :] = first
        slope1_ref[near, :] = slope1
        half2_ref[held, :] = dot(first, w2_ref[...]).astype(BF16)

    def messages(step, i):
        for j in range(i, i + OUT_MERGE):
            p = step * OUT_PAIRS + j
            near, far, held = rows(step, j, 1)
            point, slope2 = silu_pair(half2_ref[held, :])
            count = [
                jnp.full((slots, width), point_count_ref[b].astype(F32)).astype(BF16)
                for b in (p, p + half_blocks)
            ]
            mask = [jnp.clip(jnp.tile(c, (block_len // slots, 1)) - spot_ref[...], 0, 1) for c in count]
            slope2_ref[near, :] = slope2 * jnp.concatenate(mask, axis=1)
            masks = [jnp.clip(jnp.concatenate([c, c], axis=1) - lane_ref[...], 0, 1) for c in count]
            edges = [span(b * slots, slots) for b in (p, p + half_blocks)]
            send = jnp.concatenate([send_ref[e, :] * m for e, m in zip(edges, masks)], axis=0)
            ret = jnp.concatenate([ret_ref[e, :] * m for e, m in zip(edges, masks)], axis=0)
            cot = jnp.concatenate([cot_ref[near, :], cot_ref[far, :]], axis=1)
            sent = dot(send, point)
            returned = dot(ret, cot)
            mine = pl.ds(j * slots, slots)
            for side in range(2):
                lanes = slice(side * width, (side + 1) * width)
                both_ref[side, mine, :width] = sent[side * slots : (side + 1) * slots, lanes].astype(BF16)
                both_ref[side, mine, width:] = returned[side * slots : (side + 1) * slots, lanes].astype(BF16)

    def collect(step):
        for side in range(2):
            block = step * OUT_PAIRS + side * half_blocks
            select = []
            for i in range(OUT_PAIRS):
                mine = jnp.where(slot < nbr_count_ref[block + i], atoms_ref[step, side, :, i : i + 1], -1)
                select.append(jnp.where(column == mine, 1.0, 0.0).astype(BF16))
            select = jnp.concatenate(select, axis=0)
            select_ref[span(block * slots, OUT_PAIRS * slots), :] = select
            part_ref[...] += dot_rows(select, both_ref[side])

    def stages(fourth, third, second, first):
        if fourth is not None:
            collect(fourth)
        for i in range(0, OUT_PAIRS, OUT_MERGE):
            if third is not None:
                messages(third, i)
            if second is not None:
                second_layer(second, i)
            if first is not None:
                start_layer(first, i)

    def work(step, carry):
        arrive(step, points_in)
        ask(step + AHEAD, points_in)
        ask(step + 1, others_in)
        arrive(step - 2, others_in)
        stages(step - 3, step - 2, step - 1, step)
        return carry

    arrive(0, points_in)
    ask(AHEAD, points_in)
    ask(1, others_in)
    stages(None, None, None, 0)
    arrive(1, points_in)
    ask(1 + AHEAD, points_in)
    ask(2, others_in)
    stages(None, None, 0, 1)
    arrive(2, points_in)
    ask(2 + AHEAD, points_in)
    ask(3, others_in)
    arrive(0, others_in)
    stages(None, 0, 1, 2)
    lax.fori_loop(3, steps, work, 0)
    arrive(steps - 2, others_in)
    stages(steps - 3, steps - 2, steps - 1, None)
    arrive(steps - 1, others_in)
    stages(steps - 2, steps - 1, None, None)
    stages(steps - 1, None, None, None)
    part_out_ref[...] = jnp.zeros_like(part_out_ref)
    for place in range(3):
        part_out_ref[pl.ds(place * A_PAD, A_DEV), :] = part_ref[
            pl.ds(place * A_DEV, A_DEV), :
        ].astype(BF16)


def outgoing(
    first_atom, feats, cot, send, ret, neighbours, nbr_count, point_count, w_first, w_second
):
    points, width = feats.shape
    slots, blocks = neighbours.shape
    block_len = points // blocks
    steps = blocks // 2 // OUT_PAIRS
    packed = (points // 2, 2 * width)
    window = (3 * A_PAD, 2 * width)
    vmem = pl.BlockSpec(memory_space=pltpu.VMEM)
    hbm = pl.BlockSpec(memory_space=pltpu.HBM)
    inputs = (point_count, nbr_count, neighbours, feats, cot, send, ret, w_first, w_second)
    weight = pltpu.VMEM((width, width), BF16)
    weights = pltpu.VMEM((2 * width, 2 * width), BF16)

    def kernel(*refs):
        outgoing_kernel(first_atom(), *refs)

    return pl.pallas_call(
        kernel,
        in_specs=[hbm] * len(inputs),
        out_specs=[vmem] * 8,
        out_shape=[
            pltpu.VMEM(feats.shape, BF16),
            pltpu.VMEM(feats.shape, BF16),
            pltpu.VMEM(send.shape, BF16),
            pltpu.VMEM((blocks * slots, width), BF16),
            pltpu.VMEM(packed, BF16),
            pltpu.VMEM(packed, BF16),
            pltpu.VMEM(packed, BF16),
            pltpu.VMEM(window, BF16),
        ],
        scratch_shapes=[
            pltpu.VMEM(ret.shape, BF16),
            weight,
            weight,
            pltpu.VMEM(neighbours.shape, jnp.int32),
            pltpu.SMEM(point_count.shape, jnp.int32),
            pltpu.SMEM(nbr_count.shape, jnp.int32),
            weights,
            weights,
            pltpu.VMEM((block_len, width), BF16),
            pltpu.VMEM((slots, block_len), BF16),
            pltpu.VMEM((width, 2 * width), F32),
            pltpu.VMEM((steps, 2, slots, OUT_PAIRS), jnp.int32),
            pltpu.VMEM((OUT_PAIRS * block_len, 2 * width), BF16),
            pltpu.VMEM((OUT_PAIRS * block_len, 2 * width), BF16),
            pltpu.VMEM((2, OUT_PAIRS * slots, 2 * width), BF16),
            pltpu.SemaphoreType.DMA((5,)),
            pltpu.SemaphoreType.DMA((8, blocks // 2 // OUT_PAIRS)),
        ],
        compiler_params=pltpu.CompilerParams(vmem_limit_bytes=12 * 2**20),
        name="outgoing",
    )(*(pltpu.with_memory_space_constraint(value, pltpu.HBM) for value in inputs))


def incoming_kernel(
    side,
    w_second_ref,
    w_coarse_ref,
    kept_ref,
    last_ref,
    feats_ref,
    cot_ref,
    send_ref,
    select_ref,
    first_ref,
    slope1_ref,
    slope2_ref,
    dpre1_ref,
    grads_ref,
    w2_ref,
    total_ref,
    send_t_ref,
    owner_ref,
    spread_in_ref,
    held1_ref,
    dpre2_ref,
    acc1_ref,
    acc2_ref,
):
    width = feats_ref.shape[1]
    block_len = send_ref.shape[1]
    blocks = feats_ref.shape[0] // block_len
    slots = send_ref.shape[0] // blocks
    half_blocks = blocks // 2
    steps = half_blocks // IN_PAIRS

    w2_ref[...] = diag_pair(w_second_ref[...].T * 0.5)
    acc1_ref[...] = jnp.zeros_like(acc1_ref)
    acc2_ref[...] = jnp.zeros_like(acc2_ref)
    total_ref[span(side * A_PAD, A_PAD), :] = kept_ref[:A_PAD, :].astype(F32)
    total_ref[span((side + 1) * A_PAD, A_PAD), :] = kept_ref[A_PAD:, :].astype(F32)
    total_ref[span((1 - side) * 2 * A_PAD, A_PAD), :] = last_ref[...].astype(F32)
    coarse = total_ref[:, :width].astype(BF16)
    pre = dot(coarse, w_coarse_ref[...])
    sig = jax.nn.sigmoid(pre)
    slope = sig * (1.0 + pre * (1.0 - sig))
    dpre = (total_ref[:, width:] * slope).astype(BF16)
    edge_rows = IN_PAIRS * slots
    for chunk in range(2 * steps):
        send_t_ref[chunk] = send_ref[pl.ds(chunk * edge_rows, edge_rows), :].T
    owner = lax.broadcasted_iota(jnp.int32, (edge_rows, width), 0) // slots
    for place in range(IN_PAIRS):
        owner_ref[place] = jnp.where(owner == place, 1.0, 0.0).astype(BF16)
    dcoarse = dot(dpre, w_coarse_ref[...].T)
    dcoarse = [dcoarse[place * A_PAD : place * A_PAD + A_DEV] for place in range(3)]
    dcoarse.append(jnp.zeros((select_ref.shape[1] - 3 * A_DEV, width), F32))
    dcoarse = jnp.concatenate(dcoarse, axis=0).astype(BF16)
    spread_in_ref[...] = dot(select_ref[...], dcoarse).astype(BF16)
    grads_ref[2 * width :, :] = dot_rows(coarse[A_PAD : 2 * A_PAD], dpre[A_PAD : 2 * A_PAD]).astype(
        BF16
    )

    def rows(step, i, merge=IN_MERGE):
        near, far = [
            pl.ds(pl.multiple_of((step * IN_PAIRS + i + b) * block_len, block_len), merge * block_len)
            for b in (0, half_blocks)
        ]
        return near, far, pl.ds(i * block_len, merge * block_len)

    def second_grad(step, i):
        edges = [
            span((step * IN_PAIRS + half * half_blocks) * slots, IN_PAIRS * slots) for half in range(2)
        ]
        send_t = jnp.concatenate(
            [send_t_ref[step], send_t_ref[step + half_blocks // IN_PAIRS]], axis=1
        )
        for p in range(i, i + IN_MERGE):
            near, far, held = rows(step, p, 1)
            mine = [spread_in_ref[e, :] * owner_ref[p] for e in edges]
            zero = jnp.zeros_like(mine[0])
            share = jnp.concatenate(
                [jnp.concatenate([mine[0], zero], axis=1), jnp.concatenate([zero, mine[1]], axis=1)], axis=0
            )
            spread = dot(send_t, share).astype(BF16)
            cot = jnp.concatenate([cot_ref[near, :], cot_ref[far, :]], axis=1)
            dpre2_ref[held, :] = (cot + spread) * slope2_ref[near, :]

    def first_grad(step, i):
        near, _, held = rows(step, i)
        dpre2 = dpre2_ref[held, :]
        dpre1 = dot(dpre2, w2_ref[...]).astype(BF16) * slope1_ref[near, :]
        dpre1_ref[near, :] = dpre1
        held1_ref[held, :] = dpre1
        acc2_ref[...] += dot_rows(first_ref[near, :], dpre2)

    def feats_sum(step, i):
        near, far, held = rows(step, i)
        feats = jnp.concatenate([feats_ref[near, :], feats_ref[far, :]], axis=1)
        acc1_ref[...] += dot_rows(feats, held1_ref[held, :])

    def stages(third, second, first):
        for i in range(0, IN_PAIRS, IN_MERGE):
            if third is not None:
                feats_sum(third, i)
            if second is not None:
                first_grad(second, i)
            if first is not None:
                second_grad(first, i)

    def work(step, carry):
        stages(step - 2, step - 1, step)
        return carry

    stages(None, None, 0)
    stages(None, 0, 1)
    lax.fori_loop(2, steps, work, 0)
    stages(steps - 2, steps - 1, None)
    stages(steps - 1, None, None)
    for place, ref in enumerate((acc1_ref, acc2_ref)):
        grads_ref[pl.ds(place * width, width), :] = (ref[:width, :width] + ref[width:, width:]).astype(
            BF16
        )


def incoming(side, w_second, w_coarse, kept, last, resident):
    points, width = resident[0].shape
    block_len = resident[2].shape[1]
    vmem = pl.BlockSpec(memory_space=pltpu.VMEM)
    resident = [pltpu.with_memory_space_constraint(value, pltpu.VMEM) for value in resident]
    inputs = (w_second, w_coarse, kept, last, *resident)
    weights = pltpu.VMEM((2 * width, 2 * width), BF16)
    sums = pltpu.VMEM((2 * width, 2 * width), F32)
    held = pltpu.VMEM((IN_PAIRS * block_len, 2 * width), BF16)
    edge_rows = IN_PAIRS * (resident[2].shape[0] * block_len // points)

    def kernel(*refs):
        incoming_kernel(side(), *refs)

    return pl.pallas_call(
        kernel,
        in_specs=[vmem] * len(inputs),
        out_specs=[vmem, vmem],
        out_shape=[pltpu.VMEM((points // 2, 2 * width), BF16), pltpu.VMEM((3 * width, width), BF16)],
        input_output_aliases={9: 0},
        scratch_shapes=[
            weights,
            pltpu.VMEM((3 * A_PAD, 2 * width), F32),
            pltpu.VMEM((resident[2].shape[0] // edge_rows, block_len, edge_rows), BF16),
            pltpu.VMEM((IN_PAIRS, edge_rows, width), BF16),
            pltpu.VMEM((resident[2].shape[0], width), BF16),
            held,
            held,
            sums,
            sums,
        ],
        compiler_params=pltpu.CompilerParams(vmem_limit_bytes=12 * 2**20),
        name="incoming",
    )(*inputs)


def feats_grad_kernel(first, block_len, dpre1_ref, w_first_ref, *refs):
    grad_feats_hbm, stage_ref, w1_ref, sems = refs[-4:]
    width = w_first_ref.shape[0]
    half_rows = dpre1_ref.shape[0]
    rows = stage_ref.shape[1]
    w1_ref[...] = diag_pair(w_first_ref[...].T * 0.5)
    group = FEATS_GROUP * block_len
    copies = []
    for place, start in enumerate(range(0, rows, group)):
        size = min(group, rows - start)
        grad = dot(dpre1_ref[pl.ds(first + start, size), :], w1_ref[...]).astype(BF16)
        for half in range(2):
            stage_ref[half, pl.ds(start, size), :] = grad[:, half * width : (half + 1) * width]
            copies.append(
                pltpu.make_async_copy(
                    stage_ref.at[half, pl.ds(start, size), :],
                    grad_feats_hbm.at[pl.ds(half * half_rows + first + start, size), :],
                    sems.at[half, place],
                )
            )
            copies[-1].start()
    for copy in copies:
        copy.wait()


def feats_grad(first, pairs, block_len, dpre1, w_first, grad_feats):
    width = w_first.shape[0]
    half_rows = dpre1.shape[0]
    rows = pairs * block_len
    vmem = pl.BlockSpec(memory_space=pltpu.VMEM)
    hbm = pl.BlockSpec(memory_space=pltpu.HBM)
    inputs = [pltpu.with_memory_space_constraint(dpre1, pltpu.VMEM), w_first]
    if grad_feats is not None:
        inputs.append(pltpu.with_memory_space_constraint(grad_feats, pltpu.HBM))
    return pl.pallas_call(
        functools.partial(feats_grad_kernel, first * block_len, block_len),
        in_specs=[vmem, vmem, hbm][: len(inputs)],
        out_specs=hbm,
        out_shape=pltpu.HBM((2 * half_rows, width), BF16),
        input_output_aliases={} if grad_feats is None else {2: 0},
        scratch_shapes=[
            pltpu.VMEM((2, rows, width), BF16),
            pltpu.VMEM((2 * width, 2 * width), BF16),
            pltpu.SemaphoreType.DMA((2, pl.cdiv(pairs, FEATS_GROUP))),
        ],
        compiler_params=pltpu.CompilerParams(vmem_limit_bytes=12 * 2**20),
        cost_estimate=pl.CostEstimate(
            flops=4 * rows * width * width, bytes_accessed=4 * rows * width * 2, transcendentals=0
        ),
        name="feats_grad",
    )(*inputs)


def flipped(value, flip):
    count = lax.axis_size("pts")
    return lax.ppermute(value, "pts", [(i, i ^ flip) for i in range(count)])


def added(*values):
    total = values[0].astype(F32)
    for value in values[1:]:
        total = total + value.astype(F32)
    return total.astype(BF16)


def near_sums(part):
    count = lax.axis_size("pts")
    part = part.reshape(3, A_PAD, -1)
    odd = lax.rem(lax.axis_index("pts"), 2) == 1
    kept = jnp.where(odd, part[1:], part[:2])
    other = flipped(jnp.where(odd, part[0], part[2]), 1)
    inner = (lax.broadcasted_iota(jnp.int32, (2, 1, 1), 0) == 0) == odd
    kept = added(kept, jnp.where(inner, other[None], 0.0))
    steps = [(i, i + 1) for i in range(1, count - 1, 2)]
    kept = added(kept, lax.ppermute(kept, "pts", steps + [(j, i) for i, j in steps]))
    last = flipped(jnp.where(odd, kept[0], kept[1]), 1)
    return kept.reshape(2 * A_PAD, -1), last


def device_sum(value, beside):
    count = lax.axis_size("pts")
    odd = lax.rem(lax.axis_index("pts"), 2) == 1
    low, high = jnp.split(value, 2, axis=0)
    part = added(jnp.where(odd, high, low), flipped(jnp.where(odd, low, high), 1))
    place = 1
    while 2 << place <= count:
        part, result = beside(part)
        one, three, two = [flipped(part, k << place) for k in (1, 3, 2)]
        total = (part.astype(F32) + one.astype(F32)) + (two.astype(F32) + three.astype(F32))
        part = total.astype(BF16)
        part, result = lax.optimization_barrier((part, result))
        place += 2
    other = flipped(part, 1)
    return jnp.concatenate([jnp.where(odd, other, part), jnp.where(odd, part, other)], axis=0), result


def body(
    feats,
    w_first,
    w_second,
    w_coarse,
    send_weight,
    return_weight,
    neighbours,
    nbr_count,
    point_count,
    cotangent,
):
    num_blocks, num_slots, block_len = send_weight.shape
    width = feats.shape[1]
    devices = lax.axis_size("pts")
    send = send_weight.reshape(num_blocks * num_slots, block_len)
    ret = return_weight.reshape(num_blocks * num_slots, block_len)
    *resident, part = outgoing(
        lambda: (lax.axis_index("pts") - 1) * A_DEV,
        feats,
        cotangent,
        send,
        ret,
        neighbours.T,
        nbr_count,
        point_count,
        w_first,
        w_second,
    )
    kept, last = near_sums(part)
    dpre1, grads = incoming(
        lambda: lax.rem(lax.axis_index("pts"), 2), w_second, w_coarse, kept, last, resident
    )
    grad_feats = None
    done = 0
    left = list(FEATS_PARTS)

    def beside(part):
        nonlocal grad_feats, done
        held, part = lax.optimization_barrier((dpre1, part))
        size = left.pop(0)
        grad_feats = feats_grad(done, size, block_len, held, w_first, grad_feats)
        done += size
        return part, grad_feats

    grads, grad_feats = device_sum(grads, beside)
    grads = grads.astype(F32)
    total_points = devices * num_blocks * block_len
    total_atoms = devices * A_DEV
    factor = 0.5 / math.sqrt(total_points)
    return (
        grad_feats,
        grads[:width] * factor,
        grads[width : 2 * width] * factor,
        grads[2 * width :] * (1.0 / math.sqrt(total_atoms)),
    )


def solution(mesh):
    placed = (
        P("pts", None),
        P(),
        P(),
        P(),
        P("pts", None, None),
        P("pts", None, None),
        P("pts", None),
        P("pts"),
        P("pts"),
        P("pts", None),
    )
    return jax.shard_map(
        body, mesh=mesh, in_specs=placed, out_specs=(P("pts", None), P(), P(), P()), check_vma=False
    )
```
